512 devices in a mesh: src: 64 (over z_lo, x, core), gx: 2 (over z_hi), gy: 4 (over y).
Axes of the slice: x: 4, y: 4, z: 16 (z_hi: 2, z_lo: 8; z = z_hi * 8 + z_lo), core: 2. Of those that a mesh axis runs over, the one named last changes fastest.
Arguments:
- conductivity: float32 [128, 64, 128], P('gx', 'gy'), may hold values from 0.1 to 10
- potential: float32 [64, 128, 64, 128], P('src', 'gx', 'gy'), may hold values from -6 to 6
- adjoint_guess: float32 [64, 128, 64, 128], P('src', 'gx', 'gy'), may hold values from -4 to 4
- observed: float32 [64, 512], P('src'), may hold values from -6 to 6
- receiver_cells: int32 [3, 512], replicated, may hold values from 0 to 127, as said below
- electrodes: int32 [3, 64], P(None, 'src'), may hold values from 0 to 127, as said below
Outputs:
- adjoint: float32 [64, 128, 64, 128], P('src', 'gx', 'gy')
- residual_rms: float32 [64], P('src')
- gradient: float32 [128, 64, 128], P('gx', 'gy')
The draws below stay inside these ranges and needn't reach their ends.
Inputs may be any that keep to these rules, and one draw needn't show every extreme that they name: `receiver_cells`: row 0 holds x indices below 128, row 1 y indices below 64, row 2 z indices below 128. `electrodes`: row 0 holds x indices below 128, row 1 y indices below 64; row 2 is 0 (electrodes on the surface layer).
All inputs are finite; a program needn't handle non-finite values.
Results may differ from the reference program's by a relative error of at most 0.0002.
Values sent between devices are 32-bit elements; how exact they have to be, the bound alone decides.
No kernel may reach another device: no remote copies, remote signals or barrier semaphores. Data moves between devices by JAX's collectives and lax.ppermute only.
A program may use at most 64 MiB of HBM per device.

```python
import math
import jax
import jax.numpy as jnp
from jax import lax

NZ = 128
NREC = 512
SWEEPS = 4
NX = 128
NY = 64
SOURCES = 64


def draw_receiver_cells(key, part):
    key = jax.random.fold_in(key, 11)
    keys = jax.random.split(key, 3)
    first = jax.random.randint(keys[0], (NREC,), 0, NX)
    second = jax.random.randint(keys[1], (NREC,), 0, NY)
    third = jax.random.randint(keys[2], (NREC,), 0, NZ)
    cells = jnp.stack([first, second, third]).astype(jnp.int32)
    corner = jnp.array([NX - 1, NY - 1, NZ - 1], jnp.int32)
    return cells.at[:, 0].set(corner)


def draw_electrodes(key, part):
    key = jax.random.fold_in(key, 23)
    keys = jax.random.split(key, 2)
    first = jax.random.randint(keys[0], (SOURCES,), 0, NX)
    second = jax.random.randint(keys[1], (SOURCES,), 0, NY)
    cells = jnp.stack([first, second, jnp.zeros((SOURCES,), jnp.int32)]).astype(jnp.int32)
    corner = jnp.array([NX - 1, NY - 1, 0], jnp.int32)
    return cells.at[:, 0].set(corner)


def block_scale(stream_key, extent, cuts, smallest, high):
    gain, own = 1.0, jax.random.fold_in(stream_key, 6)
    for dim, blocks in cuts:
        draws = jnp.exp(jax.random.uniform(jax.random.fold_in(own, dim), (blocks,), jnp.float32, smallest / len(cuts), high / len(cuts)))
        gain = gain * jnp.repeat(draws, extent[dim] // blocks).reshape([-1 if axis == dim else 1 for axis in range(len(extent))])
    return gain


def noise(own_key, shape, spread, bound, pieces=(), dtype=jnp.bfloat16):
    factor_of = block_scale(own_key, shape, pieces, -0.22, 0.18) if pieces else 1.0
    values = jax.random.normal(own_key, shape, jnp.float32) * spread * factor_of
    return jnp.minimum(jnp.maximum(values, -bound), bound).astype(dtype)


def setup_inputs(seed: int = 0) -> dict:
    streams_of = jax.random.split(jax.random.key(seed), 7)
    return {
        "conductivity": jnp.clip(jnp.exp(math.log(10.0) - 4.6051702 * jax.random.uniform(streams_of[0], (NX, NY, NZ), jnp.float32) ** block_scale(streams_of[0], (NX, NY, NZ), ((0, 2), (1, 4)), -0.2, 0.2)), 0.1, 10.0),
        "potential": noise(streams_of[1], (SOURCES, NX, NY, NZ), 1.0, 6.0, ((0, 64), (1, 2), (2, 4)), jnp.float32),
        "adjoint_guess": noise(streams_of[2], (SOURCES, NX, NY, NZ), 0.5, 4.0, ((0, 64), (1, 2), (2, 4)), jnp.float32),
        "observed": noise(streams_of[3], (SOURCES, NREC), 1.0, 6.0, ((0, 64),), jnp.float32),
        "receiver_cells": draw_receiver_cells(jax.random.fold_in(streams_of[6], 71), 0),
        "electrodes": draw_electrodes(jax.random.fold_in(streams_of[6], 71), 0),
    }


low_bound = 0.25
high_bound = 2.0

def neighbours(padded):
    return [padded[..., 2:, 1:-1, 1:-1], padded[..., :-2, 1:-1, 1:-1], padded[..., 1:-1, 2:, 1:-1], padded[..., 1:-1, :-2, 1:-1], padded[..., 1:-1, 1:-1, 2:], padded[..., 1:-1, 1:-1, :-2]]

def apply_operator(field, face_list, diagonal):
    padded = jnp.pad(field, 1)
    total = diagonal * field
    for face, near in zip(face_list, neighbours(padded)):
        total = total - face * near
    return total

def reference(conductivity, potential, adjoint_guess, observed, receiver_cells, electrodes):
    theta = 0.5 * (high_bound + low_bound)
    delta = 0.5 * (high_bound - low_bound)
    sigma = theta / delta
    face_list = [0.5 * (conductivity + near) for near in neighbours(jnp.pad(conductivity, 1))]
    diagonal = face_list[0]
    for face in face_list[1:]:
        diagonal = diagonal + face
    rec_x = receiver_cells[0]
    rec_y = receiver_cells[1]
    rec_z = receiver_cells[2]

    def one_source(carry, item):
        field, guess, seen, electrode = item
        predicted = field[rec_x, rec_y, rec_z] - field[electrode[0], electrode[1], electrode[2]]
        misfit = predicted - seen
        adjoint_source = jnp.zeros_like(field).at[rec_x, rec_y, rec_z].add(misfit)
        adjoint_source = adjoint_source.at[electrode[0], electrode[1], electrode[2]].add(-jnp.sum(misfit))
        solution = guess
        residual = adjoint_source - apply_operator(solution, face_list, diagonal)
        direction = residual / (theta * diagonal)
        ratio = 1.0 / sigma
        for sweep in range(SWEEPS):
            solution = solution + direction
            residual = residual - apply_operator(direction, face_list, diagonal)
            if sweep < SWEEPS - 1:
                following = 1.0 / (2.0 * sigma - ratio)
                direction = following * ratio * direction + 2.0 * following / delta * residual / diagonal
                ratio = following
        rms_value = jnp.sqrt(jnp.sum(residual * residual) / (NX * NY * NZ))
        near_adj = neighbours(jnp.pad(solution, 1))
        near_pot = neighbours(jnp.pad(field, 1))
        term_cell = jnp.zeros_like(field)
        for lam_near, pot_near in zip(near_adj, near_pot):
            term_cell = term_cell - 0.5 * (solution - lam_near) * (field - pot_near)
        grad_sum, sens_sum = carry
        return ((grad_sum + term_cell, sens_sum + term_cell * term_cell), (solution, rms_value))
    start = (jnp.zeros_like(conductivity), jnp.zeros_like(conductivity))
    (grad_sum, sens_sum), (adjoint, residual_rms) = lax.scan(one_source, start, (potential, adjoint_guess, observed, jnp.transpose(electrodes)))
    gradient = grad_sum * lax.rsqrt(sens_sum / SOURCES + 1.0)
    return (adjoint, residual_rms, gradient)
```

```python
import jax
import jax.numpy as jnp
from jax import lax
from jax.experimental import pallas as pl
from jax.experimental.pallas import tpu as pltpu
from jax.sharding import PartitionSpec as P

SWEEPS = 4
LOW, HIGH = 0.25, 2.0
THETA = 0.5 * (HIGH + LOW)
DELTA = 0.5 * (HIGH - LOW)
SIGMA = THETA / DELTA

WX, WY, DEPTH = 64, 16, 128
NREC = 512
HALO = SWEEPS + 1
EX = WX + 2 * HALO
EY = WY + 16
LINE = 8
PLANE = 8
f32, bf16, i32 = jnp.float32, jnp.bfloat16, jnp.int32


def split3(value):
    top = value.astype(bf16)
    rest = value - top.astype(f32)
    middle = rest.astype(bf16)
    low = (rest - middle.astype(f32)).astype(bf16)
    return top, middle, low


def gather_kernel(rec, elec, pot, guess, cond, out):
    gx, gy = lax.axis_index("gx"), lax.axis_index("gy")
    base = jnp.where(gx == 0, WX - HALO, 0)
    for k in range(HALO):
        for half in range(2):
            out[2 * k + half] = guess[base + k, 8 * half : 8 * half + 8]
            out[10 + 2 * k + half] = cond[base + k, 8 * half : 8 * half + 8]
    face = jnp.where(gx == 0, WX - 1, 0)
    out[20] = pot[face, 0:8]
    out[21] = pot[face, 8:16]
    lx = rec[0:1, :] - gx * WX
    ly = rec[1:2, :] - gy * WY
    inside = (lx >= 0) & (lx < WX) & (ly >= 0) & (ly < WY)
    row = jnp.where(inside, lx * WY + ly, -1)
    hot = jnp.where(lax.broadcasted_iota(i32, (WX * WY, NREC), 0) == row, 1.0, 0.0).astype(bf16)
    turned = jnp.transpose(pot[...].reshape(WX * WY, DEPTH))
    parts = [jnp.dot(part, hot, preferred_element_type=f32) for part in split3(turned)]
    values = parts[0] + (parts[1] + parts[2])
    level = lax.broadcasted_iota(i32, (DEPTH, NREC), 0) == rec[2:3, :]
    picked = jnp.sum(jnp.where(level, values, 0.0), axis=0, keepdims=True)
    for k in range(NREC // DEPTH):
        out[22, k : k + 1, :] = picked[:, DEPTH * k : DEPTH * (k + 1)]
    ex = elec[0, 0] - gx * WX
    ey = elec[1, 0] - gy * WY
    held = (ex >= 0) & (ex < WX) & (ey >= 0) & (ey < WY)
    cx = jnp.clip(ex, 0, WX - 1)
    cy = jnp.clip(ey, 0, WY - 1)
    plane = pot[cx]
    here = (lax.broadcasted_iota(i32, (WY, DEPTH), 0) == cy) & (
        lax.broadcasted_iota(i32, (WY, DEPTH), 1) == elec[2, 0]
    )
    there = jnp.sum(jnp.where(here & held, plane, 0.0), axis=0, keepdims=True)
    out[22, 4:5, :] = jnp.broadcast_to(jnp.sum(there, axis=1, keepdims=True), (1, DEPTH))
    out[22, 5:8, :] = jnp.zeros((3, DEPTH), f32)


def pack_kernel(mine, theirs, pot, guess, cond, up, down, partial):
    sub = lax.broadcasted_iota(i32, (8, DEPTH), 0)

    def step(i, _):
        up[i, 0] = jnp.where(sub < 3, pltpu.roll(pot[i, 8:16], 1, 0), guess[i, 8:16])
        up[i, 1] = cond[i, 8:16]
        down[i, 0] = jnp.where(sub >= 5, pltpu.roll(pot[i, 0:8], 7, 0), guess[i, 0:8])
        down[i, 1] = cond[i, 0:8]
        return 0

    lax.fori_loop(0, WX, step, 0, unroll=4)
    for k in range(HALO):
        down[WX + k, 0] = theirs[2 * k]
        down[WX + k, 1] = theirs[10 + 2 * k]
        up[WX + k, 0] = theirs[2 * k + 1]
        up[WX + k, 1] = theirs[10 + 2 * k + 1]
    total = mine[22] + theirs[22]
    up[WX + HALO, 0] = total
    up[WX + HALO, 1] = total
    down[WX + HALO, 0] = total
    down[WX + HALO, 1] = total
    partial[...] = total


def smooth_kernel(
    rec, elec, obs, pot, guess, cond, across, from_low, from_high, own_sum, far_sum,
    adjoint, term, squares,
    c, v, r, d0, d1, fx, fy, fz, diag, inv, phi,
):
    gx, gy = lax.axis_index("gx"), lax.axis_index("gy")
    sub = lax.broadcasted_iota(i32, (8, DEPTH), 0)
    lane = lax.broadcasted_iota(i32, (EY, DEPTH), 1)
    last, first = lane == DEPTH - 1, lane == 0
    low_on, high_on = (gy > 0), (gy < lax.axis_size("gy") - 1)
    low_keep, high_keep = low_on & (sub >= 3), high_on & (sub < 5)

    def lay(i, source):
        tile = from_low[source, 0]
        v[i, 0:8] = jnp.where(low_keep, tile, 0.0)
        phi[i, 0:8] = jnp.where(low_on & (sub == 7), pltpu.roll(tile, 7, 0), 0.0)
        c[i, 0:8] = jnp.where(low_keep, from_low[source, 1], 0.0)
        tile = from_high[source, 0]
        v[i, 24:32] = jnp.where(high_keep, tile, 0.0)
        phi[i, 24:32] = jnp.where(high_on & (sub == 0), pltpu.roll(tile, 1, 0), 0.0)
        c[i, 24:32] = jnp.where(high_keep, from_high[source, 1], 0.0)

    def own(i, _):
        lay(i + HALO, i)
        v[i + HALO, 8:24] = guess[i]
        phi[i + HALO, 8:24] = pot[i]
        c[i + HALO, 8:24] = cond[i]
        return 0

    lax.fori_loop(0, WX, own, 0, unroll=2)
    blank = jnp.zeros((EY, DEPTH), f32)
    empty = jnp.where(gx == 0, 0, WX + HALO)
    there = jnp.where(gx == 0, WX + HALO, 0)
    for k in range(HALO):
        for ref in (v, phi, c):
            ref[empty + k] = blank
        lay(there + k, WX + k)
        for half in range(2):
            span = slice(8 + 8 * half, 16 + 8 * half)
            v[there + k, span] = across[2 * k + half]
            c[there + k, span] = across[10 + 2 * k + half]
            phi[there + k, span] = across[20 + half]

    def coefficients(i, _):
        here = c[i]
        fx[i] = 0.5 * (here + c[jnp.minimum(i + 1, EX - 1)])
        side = 0.5 * (here + pltpu.roll(here, EY - 1, 0))
        fy[i] = side
        near = jnp.where(last, 0.0, pltpu.roll(here, DEPTH - 1, 1))
        deep = 0.5 * (here + near)
        back = jnp.where(first, 0.5 * here, pltpu.roll(deep, 1, 1))
        fz[i] = jnp.where(last, 0.0, deep)
        before = 0.5 * (here + c[jnp.maximum(i - 1, 0)])
        total = fx[i] + before + side + pltpu.roll(side, 1, 0) + deep + back
        diag[i] = total
        inv[i] = jnp.where(here > 0.0, 1.0 / total, 0.0)
        return 0

    lax.fori_loop(0, EX, coefficients, 0, unroll=2)

    lx = rec[0:1, :] - gx * WX + HALO
    ly = rec[1:2, :] - gy * WY + 8
    near = (lx >= 0) & (lx < EX) & (ly >= 0) & (ly < EY)
    row = jnp.where(near, lx * EY + ly, -1)
    total = own_sum[...] + far_sum[...] + from_low[WX + HALO, 0] + from_high[WX + HALO, 0]
    anchor = total[4:5, :]
    pieces = [
        total[k : k + 1, :] - anchor - obs[:, DEPTH * k : DEPTH * (k + 1)]
        for k in range(NREC // DEPTH)
    ]
    misfit = jnp.concatenate(pieces, axis=1)
    whole = jnp.sum(misfit, axis=1, keepdims=True)
    level = lax.broadcasted_iota(i32, (DEPTH, NREC), 0) == rec[2:3, :]
    weights = jnp.concatenate(split3(jnp.where(level, misfit, 0.0)), axis=0)
    rows_at_once = 2

    def scatter(i, _):
        start = i * rows_at_once
        ids = lax.broadcasted_iota(i32, (rows_at_once * EY, NREC), 0) + start * EY
        hot = jnp.where(ids == row, 1.0, 0.0).astype(bf16)
        got = lax.dot_general(
            hot, weights, (((1,), (1,)), ((), ())), preferred_element_type=f32
        )
        placed = got[:, :DEPTH] + (got[:, DEPTH : 2 * DEPTH] + got[:, 2 * DEPTH :])
        r[pl.ds(start, rows_at_once)] = placed.reshape(rows_at_once, EY, DEPTH)
        return 0

    lax.fori_loop(0, EX // rows_at_once, scatter, 0)
    ex = elec[0, 0] - gx * WX + HALO
    ey = elec[1, 0] - gy * WY + 8
    held = (ex >= 0) & (ex < EX) & (ey >= 0) & (ey < EY)
    cx = jnp.clip(ex, 0, EX - 1)
    spot = (lax.broadcasted_iota(i32, (EY, DEPTH), 0) == ey) & (lane == elec[2, 0]) & held
    r[cx] = r[cx] - jnp.where(spot, whole, 0.0)

    def applied(ref, i):
        here = ref[i]
        out = diag[i] * here - fx[i] * ref[i + 1] - fx[i - 1] * ref[i - 1]
        side = fy[i]
        out = out - side * pltpu.roll(here, EY - 1, 0) - pltpu.roll(side * here, 1, 0)
        deep = fz[i]
        return out - deep * pltpu.roll(here, DEPTH - 1, 1) - pltpu.roll(deep * here, 1, 1)

    def begin(i, _):
        left = r[i] - applied(v, i)
        r[i] = left
        d0[i] = left * inv[i] * (1.0 / THETA)
        return 0

    lax.fori_loop(1, EX - 1, begin, 0, unroll=2)
    ratio = 1.0 / SIGMA
    source, target = d0, d1
    for sweep in range(SWEEPS - 1):
        following = 1.0 / (2.0 * SIGMA - ratio)
        keep, gain = following * ratio, 2.0 * following / DELTA

        def advance(i, _, source=source, target=target, keep=keep, gain=gain):
            here = source[i]
            v[i] = v[i] + here
            left = r[i] - applied(source, i)
            r[i] = left
            target[i] = keep * here + gain * (left * inv[i])
            return 0

        lax.fori_loop(2 + sweep, EX - 2 - sweep, advance, 0, unroll=2)
        ratio = following
        source, target = target, source

    v[HALO - 1] = v[HALO - 1] + source[HALO - 1]
    v[WX + HALO] = v[WX + HALO] + source[WX + HALO]

    def finish(i, acc):
        k = i + HALO
        here = source[k]
        new = v[k] + here
        v[k] = new
        adjoint[i] = new[8:24]
        left = (r[k] - applied(source, k))[8:24]
        return acc + left * left

    acc = lax.fori_loop(0, WX, finish, jnp.zeros((WY, DEPTH), f32), unroll=2)
    squares[...] = acc[0:8] + acc[8:16]

    def product(i, _):
        k = i + HALO
        a, p = v[k], phi[k]
        out = (a - v[k + 1]) * (p - phi[k + 1]) + (a - v[k - 1]) * (p - phi[k - 1])
        side = (a - pltpu.roll(a, EY - 1, 0)) * (p - pltpu.roll(p, EY - 1, 0))
        out = out + side + pltpu.roll(side, 1, 0)
        deep = (a - jnp.where(last, 0.0, pltpu.roll(a, DEPTH - 1, 1))) * (
            p - jnp.where(last, 0.0, pltpu.roll(p, DEPTH - 1, 1))
        )
        out = out + deep + jnp.where(first, a * p, pltpu.roll(deep, 1, 1))
        term[i] = -0.5 * out[8:24]
        return 0

    lax.fori_loop(0, WX, product, 0, unroll=2)


def plane_kernel(parts, own, got, out, acc):
    for q in range(LINE):
        total = parts[0, q]
        square = total * total
        for k in range(1, PLANE):
            more = parts[k, q]
            total = total + more
            square = square + more * more
        out[q, 0] = total
        out[q, 1] = square
    acc[...] = own[...] + got[...]


def scale_kernel(sources, parts, own, got, out, acc):
    total, square = parts[0, 0], parts[0, 1]
    for q in range(1, LINE):
        total = total + parts[q, 0]
        square = square + parts[q, 1]
    value = total * lax.rsqrt(square / sources + 1.0)
    for q in range(LINE):
        out[q] = value
    acc[...] = own[...] + got[...]


def spread_kernel(cells, rows, own, got, out, rms):
    value = rows[...]
    for k in range(PLANE):
        out[k] = value
    total = jnp.sum(own[...] + got[...], axis=0, keepdims=True)
    rms[...] = jnp.broadcast_to(
        jnp.sqrt(jnp.sum(total, axis=1, keepdims=True) / cells), (1, DEPTH)
    )


VM = pl.BlockSpec(memory_space=pltpu.VMEM)
SM = pl.BlockSpec(memory_space=pltpu.SMEM)


def call(kernel, shapes, specs, *args, scratch=(), flops=0, moved=0):
    return pl.pallas_call(
        kernel,
        out_shape=[jax.ShapeDtypeStruct(shape, f32) for shape in shapes],
        in_specs=specs,
        out_specs=[VM] * len(shapes),
        scratch_shapes=list(scratch),
        compiler_params=pltpu.CompilerParams(vmem_limit_bytes=48 * 1024 * 1024),
        cost_estimate=pl.CostEstimate(flops=flops, bytes_accessed=moved, transcendentals=0),
    )(*args)


def body(conductivity, potential, adjoint_guess, observed, receiver_cells, electrodes):
    sources = lax.axis_size("src")
    pot, guess = potential[0], adjoint_guess[0]
    tile = (8, DEPTH)
    swap_x = [(0, 1), (1, 0)]
    (mine,) = call(
        gather_kernel, [(23, 8, DEPTH)], [VM, SM, VM, VM, VM],
        receiver_cells, electrodes, pot, guess, conductivity,
    )
    theirs = lax.ppermute(mine, "gx", swap_x)
    faces = (WX + HALO + 1, 2, 8, DEPTH)
    up, down, partial = call(
        pack_kernel, [faces, faces, tile], [VM] * 5, mine, theirs, pot, guess, conductivity
    )
    ring = lambda step: [(i, (i + step) % 4) for i in range(4)]
    from_low = lax.ppermute(up, "gy", ring(1))
    from_high = lax.ppermute(down, "gy", ring(3))
    far = lax.ppermute(partial, "gy", ring(2))
    block = (WX, WY, DEPTH)
    adjoint, term, squares = call(
        smooth_kernel, [block, block, tile], [VM, SM] + [VM] * 9,
        receiver_cells, electrodes, observed, pot, guess, conductivity,
        theirs, from_low, from_high, partial, far,
        scratch=[pltpu.VMEM((EX, EY, DEPTH), f32)] * 11,
    )
    planes = [[z * PLANE + k for k in range(PLANE)] for z in range(LINE)]
    lines = [[z * PLANE + k for z in range(LINE)] for k in range(PLANE)]

    def exchange(value, groups):
        return lax.all_to_all(value, "src", 0, 0, axis_index_groups=groups, tiled=True)

    other = lax.ppermute(squares, "gx", swap_x)
    got = exchange(term.reshape(PLANE, LINE, WY, DEPTH), planes)
    sums, squares = call(
        plane_kernel, [(LINE, 2, WY, DEPTH), tile], [VM] * 3, got, squares, other
    )
    other = lax.ppermute(squares, "gy", [(0, 1), (1, 0), (2, 3), (3, 2)])
    got = exchange(sums, lines)
    scaled, squares = call(
        lambda *refs: scale_kernel(sources, *refs),
        [(LINE, WY, DEPTH), tile], [VM] * 3, got, squares, other,
    )
    other = lax.ppermute(squares, "gy", [(0, 2), (2, 0), (1, 3), (3, 1)])
    got = exchange(scaled, lines)
    cells = WX * lax.axis_size("gx") * WY * lax.axis_size("gy") * DEPTH
    spread, rms = call(
        lambda *refs: spread_kernel(cells, *refs),
        [(PLANE, LINE, WY, DEPTH), (1, DEPTH)], [VM] * 3, got, squares, other,
    )
    gradient = exchange(spread, planes).reshape(block)
    return adjoint[None], rms[0, :1], gradient


def solution(mesh):
    return jax.shard_map(
        body,
        mesh=mesh,
        in_specs=(
            P("gx", "gy", None),
            P("src", "gx", "gy", None),
            P("src", "gx", "gy", None),
            P("src", None),
            P(),
            P(None, "src"),
        ),
        out_specs=(P("src", "gx", "gy", None), P("src"), P("gx", "gy", None)),
        check_vma=False,
    )
```

```python
import jax
import jax.numpy as jnp
from jax import lax
from jax.experimental import pallas as pl
from jax.experimental.pallas import tpu as pltpu
from jax.sharding import PartitionSpec as P

SWEEPS = 4
LOW, HIGH = 0.25, 2.0
THETA = 0.5 * (HIGH + LOW)
DELTA = 0.5 * (HIGH - LOW)
SIGMA = THETA / DELTA

WX, WY, DEPTH = 64, 16, 128
NREC = 512
HALO = SWEEPS + 1
EX = WX + 2 * HALO
EY = WY + 16
LINE = 8
PLANE = 8
ROWS = 36
SCATTERS = 2
f32, bf16, i32 = jnp.float32, jnp.bfloat16, jnp.int32


def split3(value):
    top = value.astype(bf16)
    rest = value - top.astype(f32)
    middle = rest.astype(bf16)
    low = (rest - middle.astype(f32)).astype(bf16)
    return top, middle, low


def ahead(i):
    return pl.ds(i.start + 1, i.size)


def behind(i):
    return pl.ds(i.start - 1, i.size)


def shifted(i):
    return pl.ds(i.start - HALO, i.size)


def over_rows(low, high, step):
    count, rest = divmod(high - low, ROWS)

    def turn(k, _):
        step(pl.ds(low + k * ROWS, ROWS))
        return 0

    lax.fori_loop(0, count, turn, 0)
    if rest:
        step(pl.ds(high - rest, rest))


def gather_kernel(rec, elec, pot, guess, cond, out):
    gx, gy = lax.axis_index("gx"), lax.axis_index("gy")
    base = jnp.where(gx == 0, WX - HALO, 0)
    for k in range(HALO):
        for half in range(2):
            out[2 * k + half] = guess[base + k, 8 * half : 8 * half + 8]
            out[10 + 2 * k + half] = cond[base + k, 8 * half : 8 * half + 8]
    face = jnp.where(gx == 0, WX - 1, 0)
    out[20] = pot[face, 0:8]
    out[21] = pot[face, 8:16]
    lx = rec[0:1, :] - gx * WX
    ly = rec[1:2, :] - gy * WY
    inside = (lx >= 0) & (lx < WX) & (ly >= 0) & (ly < WY)
    row = jnp.where(inside, lx * WY + ly, -1)
    hot = jnp.where(lax.broadcasted_iota(i32, (WX * WY, NREC), 0) == row, 1.0, 0.0).astype(bf16)
    turned = jnp.transpose(pot[...].reshape(WX * WY, DEPTH))
    parts = [jnp.dot(part, hot, preferred_element_type=f32) for part in split3(turned)]
    values = parts[0] + (parts[1] + parts[2])
    level = lax.broadcasted_iota(i32, (DEPTH, NREC), 0) == rec[2:3, :]
    picked = jnp.sum(jnp.where(level, values, 0.0), axis=0, keepdims=True)
    for k in range(NREC // DEPTH):
        out[22, k : k + 1, :] = picked[:, DEPTH * k : DEPTH * (k + 1)]
    ex = elec[0, 0] - gx * WX
    ey = elec[1, 0] - gy * WY
    held = (ex >= 0) & (ex < WX) & (ey >= 0) & (ey < WY)
    cx = jnp.clip(ex, 0, WX - 1)
    cy = jnp.clip(ey, 0, WY - 1)
    plane = pot[cx]
    here = (lax.broadcasted_iota(i32, (WY, DEPTH), 0) == cy) & (
        lax.broadcasted_iota(i32, (WY, DEPTH), 1) == elec[2, 0]
    )
    there = jnp.sum(jnp.where(here & held, plane, 0.0), axis=0, keepdims=True)
    out[22, 4:5, :] = jnp.broadcast_to(jnp.sum(there, axis=1, keepdims=True), (1, DEPTH))
    out[22, 5:8, :] = jnp.zeros((3, DEPTH), f32)


def pack_kernel(mine, theirs, pot, guess, cond, up, down, partial):
    sub = lax.broadcasted_iota(i32, (8, DEPTH), 0)

    def step(i, _):
        up[i, 0] = jnp.where(sub < 3, pltpu.roll(pot[i, 8:16], 1, 0), guess[i, 8:16])
        up[i, 1] = cond[i, 8:16]
        down[i, 0] = jnp.where(sub >= 5, pltpu.roll(pot[i, 0:8], 7, 0), guess[i, 0:8])
        down[i, 1] = cond[i, 0:8]
        return 0

    lax.fori_loop(0, WX, step, 0, unroll=4)
    for k in range(HALO):
        down[WX + k, 0] = theirs[2 * k]
        down[WX + k, 1] = theirs[10 + 2 * k]
        up[WX + k, 0] = theirs[2 * k + 1]
        up[WX + k, 1] = theirs[10 + 2 * k + 1]
    total = mine[22] + theirs[22]
    up[WX + HALO, 0] = total
    up[WX + HALO, 1] = total
    down[WX + HALO, 0] = total
    down[WX + HALO, 1] = total
    partial[...] = total


def smooth_kernel(
    rec, elec, obs, pot, guess, cond, across, from_low, from_high, own_sum, far_sum,
    adjoint, term, squares,
    c, v, r, d0, d1, fx, fy, fz, diag, inv, phi,
):
    gx, gy = lax.axis_index("gx"), lax.axis_index("gy")
    sub = lax.broadcasted_iota(i32, (8, DEPTH), 0)
    low_on, high_on = (gy > 0), (gy < lax.axis_size("gy") - 1)
    low_keep, high_keep = low_on & (sub >= 3), high_on & (sub < 5)

    def lay(i, source):
        tile = from_low[source, 0]
        v[i, 0:8] = jnp.where(low_keep, tile, 0.0)
        phi[i, 0:8] = jnp.where(low_on & (sub == 7), pltpu.roll(tile, 7, 0), 0.0)
        c[i, 0:8] = jnp.where(low_keep, from_low[source, 1], 0.0)
        tile = from_high[source, 0]
        v[i, 24:32] = jnp.where(high_keep, tile, 0.0)
        phi[i, 24:32] = jnp.where(high_on & (sub == 0), pltpu.roll(tile, 1, 0), 0.0)
        c[i, 24:32] = jnp.where(high_keep, from_high[source, 1], 0.0)

    def own(i, _):
        lay(i + HALO, i)
        v[i + HALO, 8:24] = guess[i]
        phi[i + HALO, 8:24] = pot[i]
        c[i + HALO, 8:24] = cond[i]
        return 0

    lax.fori_loop(0, WX, own, 0, unroll=2)
    blank = jnp.zeros((EY, DEPTH), f32)
    empty = jnp.where(gx == 0, 0, WX + HALO)
    there = jnp.where(gx == 0, WX + HALO, 0)
    for k in range(HALO):
        for ref in (v, phi, c):
            ref[empty + k] = blank
        lay(there + k, WX + k)
        for half in range(2):
            span = slice(8 + 8 * half, 16 + 8 * half)
            v[there + k, span] = across[2 * k + half]
            c[there + k, span] = across[10 + 2 * k + half]
            phi[there + k, span] = across[20 + half]

    lane = lax.broadcasted_iota(i32, (1, EY, DEPTH), 2)
    last, first = lane == DEPTH - 1, lane == 0
    fx[0] = 0.5 * (c[0] + c[1])

    def coefficients(i):
        here = c[i]
        after = 0.5 * (here + c[ahead(i)])
        before = 0.5 * (c[behind(i)] + here)
        side = 0.5 * (here + pltpu.roll(here, EY - 1, 1))
        deep = 0.5 * (here + jnp.where(last, 0.0, pltpu.roll(here, DEPTH - 1, 2)))
        back = jnp.where(first, 0.5 * here, pltpu.roll(deep, 1, 2))
        total = after + before + side + pltpu.roll(side, 1, 1) + deep + back
        fx[i] = after
        fy[i] = side
        fz[i] = jnp.where(last, 0.0, deep)
        diag[i] = total
        inv[i] = jnp.where(here > 0.0, 1.0 / total, 0.0)

    over_rows(1, EX - 1, coefficients)

    lx = rec[0:1, :] - gx * WX + HALO
    ly = rec[1:2, :] - gy * WY + 8
    near = (lx >= 0) & (lx < EX) & (ly >= 0) & (ly < EY)
    row = jnp.where(near, lx * EY + ly, -1)
    total = own_sum[...] + far_sum[...] + from_low[WX + HALO, 0] + from_high[WX + HALO, 0]
    anchor = total[4:5, :]
    pieces = [
        total[k : k + 1, :] - anchor - obs[:, DEPTH * k : DEPTH * (k + 1)]
        for k in range(NREC // DEPTH)
    ]
    misfit = jnp.concatenate(pieces, axis=1)
    whole = jnp.sum(misfit, axis=1, keepdims=True)
    level = lax.broadcasted_iota(i32, (DEPTH, NREC), 0) == rec[2:3, :]
    weights = jnp.concatenate(split3(jnp.where(level, misfit, 0.0)), axis=0)
    span = EX // SCATTERS
    for k in range(SCATTERS):
        ids = lax.broadcasted_iota(i32, (span * EY, NREC), 0) + k * span * EY
        hot = jnp.where(ids == row, 1.0, 0.0).astype(bf16)
        got = lax.dot_general(
            hot, weights, (((1,), (1,)), ((), ())), preferred_element_type=f32
        )
        placed = got[:, :DEPTH] + (got[:, DEPTH : 2 * DEPTH] + got[:, 2 * DEPTH :])
        r[k * span : (k + 1) * span] = placed.reshape(span, EY, DEPTH)

    ex = elec[0, 0] - gx * WX + HALO
    ey = elec[1, 0] - gy * WY + 8
    held = (ex >= 0) & (ex < EX) & (ey >= 0) & (ey < EY)
    cx = jnp.clip(ex, 0, EX - 1)
    spot = (
        (lax.broadcasted_iota(i32, (EY, DEPTH), 0) == ey)
        & (lax.broadcasted_iota(i32, (EY, DEPTH), 1) == elec[2, 0])
        & held
    )
    r[cx] = r[cx] - jnp.where(spot, whole, 0.0)

    def applied(ref, i):
        here = ref[i]
        out = diag[i] * here - fx[i] * ref[ahead(i)] - fx[behind(i)] * ref[behind(i)]
        side = fy[i]
        out = out - side * pltpu.roll(here, EY - 1, 1) - pltpu.roll(side * here, 1, 1)
        deep = fz[i]
        return out - deep * pltpu.roll(here, DEPTH - 1, 2) - pltpu.roll(deep * here, 1, 2)

    def begin(i):
        left = r[i] - applied(v, i)
        r[i] = left
        d0[i] = left * inv[i] * (1.0 / THETA)

    over_rows(1, EX - 1, begin)
    ratio = 1.0 / SIGMA
    source, target = d0, d1
    for sweep in range(SWEEPS - 1):
        following = 1.0 / (2.0 * SIGMA - ratio)
        keep, gain = following * ratio, 2.0 * following / DELTA

        def advance(i, source=source, target=target, keep=keep, gain=gain):
            here = source[i]
            left = r[i] - applied(source, i)
            new = v[i] + here
            v[i] = new
            r[i] = left
            target[i] = keep * here + gain * (left * inv[i])

        over_rows(2 + sweep, EX - 2 - sweep, advance)
        ratio = following
        source, target = target, source

    v[HALO - 1] = v[HALO - 1] + source[HALO - 1]
    v[WX + HALO] = v[WX + HALO] + source[WX + HALO]
    squares[...] = jnp.zeros((8, DEPTH), f32)

    def finish(i):
        here = source[i]
        left = r[i] - applied(source, i)
        new = v[i] + here
        v[i] = new
        adjoint[shifted(i)] = new[:, 8:24]
        left = left[:, 8:24]
        left = left * left
        squares[...] += jnp.sum(left[:, :8] + left[:, 8:], axis=0)

    over_rows(HALO, WX + HALO, finish)

    def product(i):
        a, p = v[i], phi[i]
        out = (a - v[ahead(i)]) * (p - phi[ahead(i)]) + (a - v[behind(i)]) * (p - phi[behind(i)])
        side = (a - pltpu.roll(a, EY - 1, 1)) * (p - pltpu.roll(p, EY - 1, 1))
        out = out + side + pltpu.roll(side, 1, 1)
        deep = (a - jnp.where(last, 0.0, pltpu.roll(a, DEPTH - 1, 2))) * (
            p - jnp.where(last, 0.0, pltpu.roll(p, DEPTH - 1, 2))
        )
        out = out + deep + jnp.where(first, a * p, pltpu.roll(deep, 1, 2))
        term[shifted(i)] = -0.5 * out[:, 8:24]

    over_rows(HALO, WX + HALO, product)


def plane_kernel(parts, own, got, out, acc):
    for q in range(LINE):
        total = parts[0, q]
        square = total * total
        for k in range(1, PLANE):
            more = parts[k, q]
            total = total + more
            square = square + more * more
        out[q, 0] = total
        out[q, 1] = square
    acc[...] = own[...] + got[...]


def scale_kernel(sources, parts, own, got, out, acc):
    total, square = parts[0, 0], parts[0, 1]
    for q in range(1, LINE):
        total = total + parts[q, 0]
        square = square + parts[q, 1]
    value = total * lax.rsqrt(square / sources + 1.0)
    for q in range(LINE):
        out[q] = value
    acc[...] = own[...] + got[...]


def spread_kernel(cells, rows, own, got, out, rms):
    value = rows[...]
    for k in range(PLANE):
        out[k] = value
    total = jnp.sum(own[...] + got[...], axis=0, keepdims=True)
    rms[...] = jnp.broadcast_to(
        jnp.sqrt(jnp.sum(total, axis=1, keepdims=True) / cells), (1, DEPTH)
    )


VM = pl.BlockSpec(memory_space=pltpu.VMEM)
SM = pl.BlockSpec(memory_space=pltpu.SMEM)


def call(kernel, shapes, specs, *args, scratch=(), flops=0, moved=0):
    return pl.pallas_call(
        kernel,
        out_shape=[jax.ShapeDtypeStruct(shape, f32) for shape in shapes],
        in_specs=specs,
        out_specs=[VM] * len(shapes),
        scratch_shapes=list(scratch),
        compiler_params=pltpu.CompilerParams(vmem_limit_bytes=48 * 1024 * 1024),
        cost_estimate=pl.CostEstimate(flops=flops, bytes_accessed=moved, transcendentals=0),
    )(*args)


def body(conductivity, potential, adjoint_guess, observed, receiver_cells, electrodes):
    sources = lax.axis_size("src")
    pot, guess = potential[0], adjoint_guess[0]
    tile = (8, DEPTH)
    swap_x = [(0, 1), (1, 0)]
    (mine,) = call(
        gather_kernel, [(23, 8, DEPTH)], [VM, SM, VM, VM, VM],
        receiver_cells, electrodes, pot, guess, conductivity,
    )
    theirs = lax.ppermute(mine, "gx", swap_x)
    faces = (WX + HALO + 1, 2, 8, DEPTH)
    up, down, partial = call(
        pack_kernel, [faces, faces, tile], [VM] * 5, mine, theirs, pot, guess, conductivity
    )
    ring = lambda step: [(i, (i + step) % 4) for i in range(4)]
    from_low = lax.ppermute(up, "gy", ring(1))
    from_high = lax.ppermute(down, "gy", ring(3))
    far = lax.ppermute(partial, "gy", ring(2))
    block = (WX, WY, DEPTH)
    adjoint, term, squares = call(
        smooth_kernel, [block, block, tile], [VM, SM] + [VM] * 9,
        receiver_cells, electrodes, observed, pot, guess, conductivity,
        theirs, from_low, from_high, partial, far,
        scratch=[pltpu.VMEM((EX, EY, DEPTH), f32)] * 11,
    )
    planes = [[z * PLANE + k for k in range(PLANE)] for z in range(LINE)]
    lines = [[z * PLANE + k for z in range(LINE)] for k in range(PLANE)]

    def exchange(value, groups):
        return lax.all_to_all(value, "src", 0, 0, axis_index_groups=groups, tiled=True)

    other = lax.ppermute(squares, "gx", swap_x)
    got = exchange(term.reshape(PLANE, LINE, WY, DEPTH), planes)
    sums, squares = call(
        plane_kernel, [(LINE, 2, WY, DEPTH), tile], [VM] * 3, got, squares, other
    )
    other = lax.ppermute(squares, "gy", [(0, 1), (1, 0), (2, 3), (3, 2)])
    got = exchange(sums, lines)
    scaled, squares = call(
        lambda *refs: scale_kernel(sources, *refs),
        [(LINE, WY, DEPTH), tile], [VM] * 3, got, squares, other,
    )
    other = lax.ppermute(squares, "gy", [(0, 2), (2, 0), (1, 3), (3, 1)])
    got = exchange(scaled, lines)
    cells = WX * lax.axis_size("gx") * WY * lax.axis_size("gy") * DEPTH
    spread, rms = call(
        lambda *refs: spread_kernel(cells, *refs),
        [(PLANE, LINE, WY, DEPTH), (1, DEPTH)], [VM] * 3, got, squares, other,
    )
    gradient = exchange(spread, planes).reshape(block)
    return adjoint[None], rms[0, :1], gradient


def solution(mesh):
    return jax.shard_map(
        body,
        mesh=mesh,
        in_specs=(
            P("gx", "gy", None),
            P("src", "gx", "gy", None),
            P("src", "gx", "gy", None),
            P("src", None),
            P(),
            P(None, "src"),
        ),
        out_specs=(P("src", "gx", "gy", None), P("src"), P("gx", "gy", None)),
        check_vma=False,
    )
```

```python
import jax
import jax.numpy as jnp
from jax import lax
from jax.experimental import pallas as pl
from jax.experimental.pallas import tpu as pltpu
from jax.sharding import PartitionSpec as P

SWEEPS = 4
LOW, HIGH = 0.25, 2.0
THETA = 0.5 * (HIGH + LOW)
DELTA = 0.5 * (HIGH - LOW)
SIGMA = THETA / DELTA

WX, WY, DEPTH = 64, 16, 128
NREC = 512
HALO = SWEEPS + 1
EX = WX + 2 * HALO
EY = WY + 16
LINE = 8
PLANE = 8
ROWS = 36
SCATTERS = 2
LOADS = 8
GRANT = 63_800_000
f32, bf16, i32 = jnp.float32, jnp.bfloat16, jnp.int32


def split3(value):
    top = value.astype(bf16)
    rest = value - top.astype(f32)
    middle = rest.astype(bf16)
    low = (rest - middle.astype(f32)).astype(bf16)
    return top, middle, low


def ahead(i):
    return pl.ds(i.start + 1, i.size)


def behind(i):
    return pl.ds(i.start - 1, i.size)


def shifted(i):
    return pl.ds(i.start - HALO, i.size)


def over_rows(low, high, step):
    count, rest = divmod(high - low, ROWS)

    def turn(k, _):
        step(pl.ds(low + k * ROWS, ROWS))
        return 0

    lax.fori_loop(0, count, turn, 0)
    if rest:
        step(pl.ds(high - rest, rest))


def gather_kernel(elec, rec_in, pot_in, guess, cond, out, rec, pot, sems):
    gx, gy = lax.axis_index("gx"), lax.axis_index("gy")
    base = jnp.where(gx == 0, WX - HALO, 0)
    step = WX // LOADS
    pairs = [(rec_in, rec)]
    for k in range(LOADS):
        pairs.append((pot_in.at[pl.ds(k * step, step)], pot.at[pl.ds(k * step, step)]))
    pairs.append((guess.at[pl.ds(base, HALO)], out.at[pl.ds(0, HALO)]))
    pairs.append((cond.at[pl.ds(base, HALO)], out.at[pl.ds(HALO, HALO)]))
    loads = [
        pltpu.make_async_copy(source, target, sems.at[k])
        for k, (source, target) in enumerate(pairs)
    ]
    for load in loads:
        load.start()
    loads[0].wait()
    lx = rec[0:1, :] - gx * WX
    ly = rec[1:2, :] - gy * WY
    inside = (lx >= 0) & (lx < WX) & (ly >= 0) & (ly < WY)
    row = jnp.where(inside, lx * WY + ly, -1)
    hot = jnp.where(lax.broadcasted_iota(i32, (WX * WY, NREC), 0) == row, 1.0, 0.0).astype(bf16)
    for load in loads[1:]:
        load.wait()
    turned = jnp.transpose(pot[...].reshape(WX * WY, DEPTH))
    parts = [jnp.dot(part, hot, preferred_element_type=f32) for part in split3(turned)]
    values = parts[0] + (parts[1] + parts[2])
    level = lax.broadcasted_iota(i32, (DEPTH, NREC), 0) == rec[2:3, :]
    picked = jnp.sum(jnp.where(level, values, 0.0), axis=0, keepdims=True)
    for k in range(NREC // DEPTH):
        out[2 * HALO + 1, k : k + 1, :] = picked[:, DEPTH * k : DEPTH * (k + 1)]
    ex = elec[0, 0] - gx * WX
    ey = elec[0, 1] - gy * WY
    held = (ex >= 0) & (ex < WX) & (ey >= 0) & (ey < WY)
    cx = jnp.clip(ex, 0, WX - 1)
    cy = jnp.clip(ey, 0, WY - 1)
    plane = pot[cx]
    here = (lax.broadcasted_iota(i32, (WY, DEPTH), 0) == cy) & (
        lax.broadcasted_iota(i32, (WY, DEPTH), 1) == elec[0, 2]
    )
    there = jnp.sum(jnp.where(here & held, plane, 0.0), axis=0, keepdims=True)
    value = jnp.sum(there, axis=1, keepdims=True)
    out[2 * HALO + 1, 4:5, :] = jnp.broadcast_to(value, (1, DEPTH))
    out[2 * HALO + 1, 5:16, :] = jnp.zeros((11, DEPTH), f32)
    out[2 * HALO] = pot[jnp.where(gx == 0, WX - 1, 0)]


def spare(n):
    return WX // 2 + n // 3, n % 3


def pack_kernel(mine, theirs, pot, guess, cond, up, down, partial):
    sub = lax.broadcasted_iota(i32, (1, 8, DEPTH), 1)
    own = slice(0, WX // 2)
    for out, span, keep, turn in ((up, slice(8, 16), sub >= 3, 3), (down, slice(0, 8), sub < 5, 7)):
        g, p, c = (ref[:, span].reshape(WX // 2, 2, 8, DEPTH) for ref in (guess, pot, cond))
        at_pot = sub == (2 if turn == 3 else 7)
        roll = lambda value, by: pltpu.roll(value, by, 1)
        rest = jnp.where(at_pot, roll(p[:, 0], turn), roll(c[:, 1], 2))
        out[own, 0] = jnp.where(keep, g[:, 0], roll(c[:, 1], 5))
        out[own, 1] = jnp.where(keep, g[:, 1], rest)
        out[own, 2] = jnp.where(keep, c[:, 0], roll(p[:, 1], turn))
    total = mine[2 * HALO + 1, 0:8] + theirs[2 * HALO + 1, 0:8]
    for n in range(2 * HALO):
        down[spare(n)] = theirs[n, 0:8]
        up[spare(n)] = theirs[n, 8:16]
    for n in range(2 * HALO, 12):
        up[spare(n)] = total
        down[spare(n)] = total
    partial[...] = total


def smooth_kernel(
    rec, elec, obs, pot, guess, cond, across, from_low, from_high, own_sum, far_sum,
    adjoint, term, squares,
    c, v, r, d0, d1, fx, fy, fz, diag, inv, phi, final, sem,
):
    gx, gy = lax.axis_index("gx"), lax.axis_index("gy")
    sub = lax.broadcasted_iota(i32, (8, DEPTH), 0)
    low_on, high_on = (gy > 0), (gy < lax.axis_size("gy") - 1)
    low_keep, high_keep = low_on & (sub >= 3), high_on & (sub < 5)
    roll = lambda value, by: pltpu.roll(value, by, 0)

    def own(i, _):
        x = 2 * i + HALO
        first, second, third = from_low[i, 0], from_low[i, 1], from_low[i, 2]
        mixed = jnp.where(sub >= 6, roll(second, 6), roll(first, 3))
        v[x, 0:8] = jnp.where(low_keep, first, 0.0)
        v[x + 1, 0:8] = jnp.where(low_keep, second, 0.0)
        c[x, 0:8] = jnp.where(low_keep, third, 0.0)
        c[x + 1, 0:8] = jnp.where(low_keep, mixed, 0.0)
        phi[x, 0:8] = jnp.where(low_keep, roll(second, 5), 0.0)
        phi[x + 1, 0:8] = jnp.where(low_keep, roll(third, 5), 0.0)
        first, second, third = from_high[i, 0], from_high[i, 1], from_high[i, 2]
        mixed = jnp.where(sub < 3, roll(first, 3), roll(second, 6))
        v[x, 24:32] = jnp.where(high_keep, first, 0.0)
        v[x + 1, 24:32] = jnp.where(high_keep, second, 0.0)
        c[x, 24:32] = jnp.where(high_keep, third, 0.0)
        c[x + 1, 24:32] = jnp.where(high_keep, mixed, 0.0)
        phi[x, 24:32] = jnp.where(high_keep, roll(second, 1), 0.0)
        phi[x + 1, 24:32] = jnp.where(high_keep, roll(third, 1), 0.0)
        for k in range(2):
            v[x + k, 8:24] = guess[2 * i + k]
            phi[x + k, 8:24] = pot[2 * i + k]
            c[x + k, 8:24] = cond[2 * i + k]
        return 0

    lax.fori_loop(0, WX // 2, own, 0, unroll=2)
    blank = jnp.zeros((EY, DEPTH), f32)
    empty = jnp.where(gx == 0, 0, WX + HALO)
    there = jnp.where(gx == 0, WX + HALO, 0)
    for k in range(HALO):
        for ref in (v, phi, c):
            ref[empty + k] = blank
        for ref, n in ((v, k), (c, HALO + k)):
            ref[there + k, 0:8] = jnp.where(low_keep, from_low[spare(n)], 0.0)
            ref[there + k, 8:24] = across[n]
            ref[there + k, 24:32] = jnp.where(high_keep, from_high[spare(n)], 0.0)
        phi[there + k] = blank
    phi[jnp.where(gx == 0, WX + HALO, HALO - 1), 8:24] = across[2 * HALO]

    lane = lax.broadcasted_iota(i32, (1, EY, DEPTH), 2)
    last, first = lane == DEPTH - 1, lane == 0
    fx[0] = 0.5 * (c[0] + c[1])

    def coefficients(i):
        here = c[i]
        after = 0.5 * (here + c[ahead(i)])
        before = 0.5 * (c[behind(i)] + here)
        side = 0.5 * (here + pltpu.roll(here, EY - 1, 1))
        deep = 0.5 * (here + jnp.where(last, 0.0, pltpu.roll(here, DEPTH - 1, 2)))
        back = jnp.where(first, 0.5 * here, pltpu.roll(deep, 1, 2))
        total = after + before + side + pltpu.roll(side, 1, 1) + deep + back
        fx[i] = after
        fy[i] = side
        fz[i] = jnp.where(last, 0.0, deep)
        diag[i] = total
        inv[i] = jnp.where(here > 0.0, 1.0 / total, 0.0)

    over_rows(1, EX - 1, coefficients)

    lx = rec[0:1, :] - gx * WX + HALO
    ly = rec[1:2, :] - gy * WY + 8
    near = (lx >= 0) & (lx < EX) & (ly >= 0) & (ly < EY)
    row = jnp.where(near, lx * EY + ly, -1)
    total = own_sum[...] + far_sum[...] + from_low[spare(2 * HALO)] + from_high[spare(2 * HALO)]
    anchor = total[4:5, :]
    pieces = [
        total[k : k + 1, :] - anchor - obs[:, DEPTH * k : DEPTH * (k + 1)]
        for k in range(NREC // DEPTH)
    ]
    misfit = jnp.concatenate(pieces, axis=1)
    whole = jnp.sum(misfit, axis=1, keepdims=True)
    level = lax.broadcasted_iota(i32, (DEPTH, NREC), 0) == rec[2:3, :]
    weights = jnp.concatenate(split3(jnp.where(level, misfit, 0.0)), axis=0)
    span = EX // SCATTERS
    for k in range(SCATTERS):
        ids = lax.broadcasted_iota(i32, (span * EY, NREC), 0) + k * span * EY
        hot = jnp.where(ids == row, 1.0, 0.0).astype(bf16)
        got = lax.dot_general(
            hot, weights, (((1,), (1,)), ((), ())), preferred_element_type=f32
        )
        placed = got[:, :DEPTH] + (got[:, DEPTH : 2 * DEPTH] + got[:, 2 * DEPTH :])
        r[k * span : (k + 1) * span] = placed.reshape(span, EY, DEPTH)

    ex = elec[0, 0] - gx * WX + HALO
    ey = elec[0, 1] - gy * WY + 8
    held = (ex >= 0) & (ex < EX) & (ey >= 0) & (ey < EY)
    cx = jnp.clip(ex, 0, EX - 1)
    spot = (
        (lax.broadcasted_iota(i32, (EY, DEPTH), 0) == ey)
        & (lax.broadcasted_iota(i32, (EY, DEPTH), 1) == elec[0, 2])
        & held
    )
    r[cx] = r[cx] - jnp.where(spot, whole, 0.0)

    def applied(ref, i):
        here = ref[i]
        out = diag[i] * here - fx[i] * ref[ahead(i)] - fx[behind(i)] * ref[behind(i)]
        side = fy[i]
        out = out - side * pltpu.roll(here, EY - 1, 1) - pltpu.roll(side * here, 1, 1)
        deep = fz[i]
        return out - deep * pltpu.roll(here, DEPTH - 1, 2) - pltpu.roll(deep * here, 1, 2)

    def begin(i):
        left = r[i] - applied(v, i)
        r[i] = left
        d0[i] = left * inv[i] * (1.0 / THETA)

    over_rows(1, EX - 1, begin)
    ratio = 1.0 / SIGMA
    source, target = d0, d1
    for sweep in range(SWEEPS - 1):
        following = 1.0 / (2.0 * SIGMA - ratio)
        keep, gain = following * ratio, 2.0 * following / DELTA

        def advance(i, source=source, target=target, keep=keep, gain=gain):
            here = source[i]
            left = r[i] - applied(source, i)
            new = v[i] + here
            v[i] = new
            r[i] = left
            target[i] = keep * here + gain * (left * inv[i])

        over_rows(2 + sweep, EX - 2 - sweep, advance)
        ratio = following
        source, target = target, source

    v[HALO - 1] = v[HALO - 1] + source[HALO - 1]
    v[WX + HALO] = v[WX + HALO] + source[WX + HALO]
    squares[...] = jnp.zeros((8, DEPTH), f32)

    def finish(i):
        here = source[i]
        left = r[i] - applied(source, i)
        new = v[i] + here
        v[i] = new
        final[shifted(i)] = new[:, 8:24]
        left = left[:, 8:24]
        left = left * left
        squares[...] += jnp.sum(left[:, :8] + left[:, 8:], axis=0)

    over_rows(HALO, WX + HALO, finish)
    store = pltpu.make_async_copy(final, adjoint, sem)
    store.start()

    def product(i):
        a, p = v[i], phi[i]
        out = (a - v[ahead(i)]) * (p - phi[ahead(i)]) + (a - v[behind(i)]) * (p - phi[behind(i)])
        side = (a - pltpu.roll(a, EY - 1, 1)) * (p - pltpu.roll(p, EY - 1, 1))
        out = out + side + pltpu.roll(side, 1, 1)
        deep = (a - jnp.where(last, 0.0, pltpu.roll(a, DEPTH - 1, 2))) * (
            p - jnp.where(last, 0.0, pltpu.roll(p, DEPTH - 1, 2))
        )
        out = out + deep + jnp.where(first, a * p, pltpu.roll(deep, 1, 2))
        term[shifted(i)] = -0.5 * out[:, 8:24]

    over_rows(HALO, WX + HALO, product)
    store.wait()


def plane_kernel(parts, own, got, out, acc):
    for q in range(LINE):
        total = parts[0, q]
        square = total * total
        for k in range(1, PLANE):
            more = parts[k, q]
            total = total + more
            square = square + more * more
        out[q, 0] = total
        out[q, 1] = square
    acc[...] = own[...] + got[...]


def scale_kernel(sources, parts, out):
    total, square = parts[0, 0], parts[0, 1]
    for q in range(1, LINE):
        total = total + parts[q, 0]
        square = square + parts[q, 1]
    value = total * lax.rsqrt(square / sources + 1.0)
    for q in range(LINE):
        out[q] = value


def spread_kernel(rows, own, got, out, acc):
    value = rows[...]
    for k in range(PLANE):
        out[k] = value
    acc[...] = own[...] + got[...]


def rms_kernel(cells, own, got, rms):
    total = jnp.sum(own[...] + got[...], axis=0, keepdims=True)
    rms[...] = jnp.broadcast_to(
        jnp.sqrt(jnp.sum(total, axis=1, keepdims=True) / cells), (1, DEPTH)
    )


VM = pl.BlockSpec(memory_space=pltpu.VMEM)
SM = pl.BlockSpec(memory_space=pltpu.SMEM)
HB = pl.BlockSpec(memory_space=pl.ANY)


def call(kernel, shapes, specs, *args, scratch=(), limit=48 * 1024 * 1024, outs=None):
    return pl.pallas_call(
        kernel,
        out_shape=[jax.ShapeDtypeStruct(shape, f32) for shape in shapes],
        in_specs=specs,
        out_specs=outs or [VM] * len(shapes),
        scratch_shapes=list(scratch),
        compiler_params=pltpu.CompilerParams(vmem_limit_bytes=limit),
    )(*args)


def body(conductivity, potential, adjoint_guess, observed, receiver_cells, electrodes):
    sources = lax.axis_size("src")
    pot, guess = potential[0], adjoint_guess[0]
    elec = jnp.transpose(electrodes)
    tile = (8, DEPTH)
    swap_x = [(0, 1), (1, 0)]
    (mine,) = call(
        gather_kernel, [(2 * HALO + 2, WY, DEPTH)], [SM, HB, HB, HB, HB],
        elec, receiver_cells, pot, guess, conductivity,
        scratch=[
            pltpu.VMEM((3, NREC), i32),
            pltpu.VMEM((WX, WY, DEPTH), f32),
            pltpu.SemaphoreType.DMA((3 + LOADS,)),
        ],
        limit=GRANT,
    )
    theirs = lax.ppermute(mine, "gx", swap_x)
    faces = (WX // 2 + 4, 3, 8, DEPTH)
    up, down, partial = call(
        pack_kernel, [faces, faces, tile], [VM] * 5, mine, theirs, pot, guess, conductivity
    )
    ring = lambda step: [(i, (i + step) % 4) for i in range(4)]
    from_low = lax.ppermute(up, "gy", ring(1))
    from_high = lax.ppermute(down, "gy", ring(3))
    far = lax.ppermute(partial, "gy", ring(2))
    block = (WX, WY, DEPTH)
    adjoint, term, squares = call(
        smooth_kernel, [block, block, tile], [VM, SM] + [VM] * 9,
        receiver_cells, elec, observed, pot, guess, conductivity,
        theirs, from_low, from_high, partial, far,
        scratch=[pltpu.VMEM((EX, EY, DEPTH), f32)] * 11
        + [pltpu.VMEM(block, f32), pltpu.SemaphoreType.DMA],
        outs=[HB, VM, VM],
    )
    planes = [[z * PLANE + k for k in range(PLANE)] for z in range(LINE)]
    lines = [[z * PLANE + k for z in range(LINE)] for k in range(PLANE)]

    def exchange(value, groups):
        return lax.all_to_all(value, "src", 0, 0, axis_index_groups=groups, tiled=True)

    other = lax.ppermute(squares, "gx", swap_x)
    got = exchange(term.reshape(PLANE, LINE, WY, DEPTH), planes)
    sums, squares = call(
        plane_kernel, [(LINE, 2, WY, DEPTH), tile], [VM] * 3, got, squares, other
    )
    got = exchange(sums, lines)
    (scaled,) = call(
        lambda *refs: scale_kernel(sources, *refs), [(LINE, WY, DEPTH)], [VM], got
    )
    other = lax.ppermute(squares, "gy", [(0, 1), (1, 0), (2, 3), (3, 2)])
    got = exchange(scaled, lines)
    spread, squares = call(
        spread_kernel, [(PLANE, LINE, WY, DEPTH), tile], [VM] * 3, got, squares, other
    )
    other = lax.ppermute(squares, "gy", [(0, 2), (2, 0), (1, 3), (3, 1)])
    gradient = exchange(spread, planes).reshape(block)
    cells = WX * lax.axis_size("gx") * WY * lax.axis_size("gy") * DEPTH
    (rms,) = call(
        lambda *refs: rms_kernel(cells, *refs), [(1, DEPTH)], [VM] * 2, squares, other
    )
    return adjoint[None], rms[0, :1], gradient


def solution(mesh):
    return jax.shard_map(
        body,
        mesh=mesh,
        in_specs=(
            P("gx", "gy", None),
            P("src", "gx", "gy", None),
            P("src", "gx", "gy", None),
            P("src", None),
            P(),
            P(None, "src"),
        ),
        out_specs=(P("src", "gx", "gy", None), P("src"), P("gx", "gy", None)),
        check_vma=False,
    )
```

```python
import jax
import jax.numpy as jnp
from jax import lax
from jax.experimental import pallas as pl
from jax.experimental.pallas import tpu as pltpu
from jax.sharding import PartitionSpec as P

SWEEPS = 4
LOW, HIGH = 0.25, 2.0
THETA = 0.5 * (HIGH + LOW)
DELTA = 0.5 * (HIGH - LOW)
SIGMA = THETA / DELTA

WX, WY, DEPTH = 64, 16, 128
NREC = 512
HALO = SWEEPS + 1
EX = WX + 2 * HALO
EY = WY + 16
LINE = 8
PLANE = 8
ROWS = 36
SCATTERS = 2
LOADS = 8
GRANT = 63_800_000
f32, bf16, i32 = jnp.float32, jnp.bfloat16, jnp.int32


def split3(value):
    top = value.astype(bf16)
    rest = value - top.astype(f32)
    middle = rest.astype(bf16)
    low = (rest - middle.astype(f32)).astype(bf16)
    return top, middle, low


def ahead(i):
    return pl.ds(i.start + 1, i.size)


def behind(i):
    return pl.ds(i.start - 1, i.size)


def shifted(i):
    return pl.ds(i.start - HALO, i.size)


def over_rows(low, high, step):
    count, rest = divmod(high - low, ROWS)

    def turn(k, _):
        step(pl.ds(low + k * ROWS, ROWS))
        return 0

    lax.fori_loop(0, count, turn, 0)
    if rest:
        step(pl.ds(high - rest, rest))


def sides(gy):
    return gy > 0, gy < lax.axis_size("gy") - 1


def corner(near, low):
    sub = lax.broadcasted_iota(i32, (8, DEPTH), 0)
    tiles = []
    for n in range(2):
        if low:
            second = jnp.where(sub == 0, pltpu.roll(near(n, 4), 1, 0), pltpu.roll(near(n, 2), 4, 0))
            tiles.append(jnp.where(sub >= 4, near(n, 1), second))
        else:
            second = jnp.where(sub == 7, pltpu.roll(near(n, 4), 7, 0), pltpu.roll(near(n, 2), 4, 0))
            tiles.append(jnp.where(sub < 4, near(n, 1), second))
    if low:
        tiles.append(jnp.where(sub >= 6, near(0, 3), pltpu.roll(near(1, 3), 6, 0)))
    else:
        tiles.append(jnp.where(sub < 2, near(0, 3), pltpu.roll(near(1, 3), 2, 0)))
    return tiles


def uncorner(tiles, low):
    sub = lax.broadcasted_iota(i32, (8, DEPTH), 0)
    out = {}
    for n in range(2):
        if low:
            out[n, 1] = jnp.where(sub >= 4, tiles[n], 0.0)
            out[n, 2] = jnp.where(sub >= 5, pltpu.roll(tiles[n], 4, 0), 0.0)
            out[n, 3] = jnp.where(sub >= 6, pltpu.roll(tiles[2], 2 * n, 0) if n else tiles[2], 0.0)
            out[n, 4] = jnp.where(sub == 7, pltpu.roll(tiles[n], 7, 0), 0.0)
        else:
            out[n, 1] = jnp.where(sub < 4, tiles[n], 0.0)
            out[n, 2] = jnp.where(sub < 3, pltpu.roll(tiles[n], 4, 0), 0.0)
            out[n, 3] = jnp.where(sub < 2, pltpu.roll(tiles[2], 6, 0) if n else tiles[2], 0.0)
            out[n, 4] = jnp.where(sub == 0, pltpu.roll(tiles[n], 1, 0), 0.0)
    return out


def gather_kernel(elec, rec_in, pot_in, guess, cond, out, rec, pot, sems):
    gx, gy = lax.axis_index("gx"), lax.axis_index("gy")
    base = jnp.where(gx == 0, WX - HALO, 0)
    step = WX // LOADS
    pairs = [(rec_in, rec)]
    for k in range(LOADS):
        pairs.append((pot_in.at[pl.ds(k * step, step)], pot.at[pl.ds(k * step, step)]))
    pairs.append((guess.at[pl.ds(base, HALO)], out.at[pl.ds(0, HALO)]))
    pairs.append((cond.at[pl.ds(base, HALO)], out.at[pl.ds(HALO, HALO)]))
    loads = [
        pltpu.make_async_copy(source, target, sems.at[k])
        for k, (source, target) in enumerate(pairs)
    ]
    for load in loads:
        load.start()
    loads[0].wait()
    lx = rec[0:1, :] - gx * WX
    ly = rec[1:2, :] - gy * WY
    inside = (lx >= 0) & (lx < WX) & (ly >= 0) & (ly < WY)
    row = jnp.where(inside, lx * WY + ly, -1)
    hot = jnp.where(lax.broadcasted_iota(i32, (WX * WY, NREC), 0) == row, 1.0, 0.0).astype(bf16)
    for load in loads[1:]:
        load.wait()
    turned = jnp.transpose(pot[...].reshape(WX * WY, DEPTH))
    parts = [jnp.dot(part, hot, preferred_element_type=f32) for part in split3(turned)]
    values = parts[0] + (parts[1] + parts[2])
    level = lax.broadcasted_iota(i32, (DEPTH, NREC), 0) == rec[2:3, :]
    picked = jnp.sum(jnp.where(level, values, 0.0), axis=0, keepdims=True)
    for k in range(NREC // DEPTH):
        out[2 * HALO + 1, k : k + 1, :] = picked[:, DEPTH * k : DEPTH * (k + 1)]
    ex = elec[0, 0] - gx * WX
    ey = elec[0, 1] - gy * WY
    held = (ex >= 0) & (ex < WX) & (ey >= 0) & (ey < WY)
    cx = jnp.clip(ex, 0, WX - 1)
    cy = jnp.clip(ey, 0, WY - 1)
    plane = pot[cx]
    here = (lax.broadcasted_iota(i32, (WY, DEPTH), 0) == cy) & (
        lax.broadcasted_iota(i32, (WY, DEPTH), 1) == elec[0, 2]
    )
    there = jnp.sum(jnp.where(here & held, plane, 0.0), axis=0, keepdims=True)
    value = jnp.sum(there, axis=1, keepdims=True)
    out[2 * HALO + 1, 4:5, :] = jnp.broadcast_to(value, (1, DEPTH))
    out[2 * HALO + 1, 5:16, :] = jnp.zeros((11, DEPTH), f32)
    out[2 * HALO] = pot[jnp.where(gx == 0, WX - 1, 0)]


def pack_kernel(mine, pot, guess, cond, up, down, partial, sem):
    load = pltpu.make_async_copy(mine.at[2 * HALO + 1, pl.ds(0, 8)], partial, sem)
    load.start()
    sub = lax.broadcasted_iota(i32, (1, 8, DEPTH), 1)
    for out, span, keep, turn in ((up, slice(8, 16), sub >= 3, 3), (down, slice(0, 8), sub < 5, 7)):
        g, p, c = (ref[:, span].reshape(WX // 2, 2, 8, DEPTH) for ref in (guess, pot, cond))
        at_pot = sub == (2 if turn == 3 else 7)
        roll = lambda value, by: pltpu.roll(value, by, 1)
        rest = jnp.where(at_pot, roll(p[:, 0], turn), roll(c[:, 1], 2))
        out[:, 0] = jnp.where(keep, g[:, 0], roll(c[:, 1], 5))
        out[:, 1] = jnp.where(keep, g[:, 1], rest)
        out[:, 2] = jnp.where(keep, c[:, 0], roll(p[:, 1], turn))
    load.wait()


def corner_kernel(own, theirs, spots):
    gx, gy = lax.axis_index("gx"), lax.axis_index("gy")

    def near(half):
        def tile(n, k):
            x = n * HALO + jnp.where(gx == 0, k - 1, HALO - k)
            return theirs[x, 8 * half : 8 * half + 8]

        return tile

    count = spots.shape[0]
    total = own[...] + theirs[2 * HALO + 1, 0:8]
    high, low = corner(near(1), True), corner(near(0), False)
    for j in range(count):
        for k in range(3):
            spots[j, k] = jnp.where(j > gy, high[k], low[k])
        spots[j, 3] = total


def smooth_kernel(
    rec, elec, obs, pot, guess, cond, across, from_low, from_high, spots,
    adjoint, term, squares,
    c, v, r, d0, d1, fx, fy, fz, diag, inv, phi, final, sem,
):
    gx, gy = lax.axis_index("gx"), lax.axis_index("gy")
    sub = lax.broadcasted_iota(i32, (8, DEPTH), 0)
    low_on, high_on = (gy > 0), (gy < lax.axis_size("gy") - 1)
    low_keep, high_keep = low_on & (sub >= 3), high_on & (sub < 5)
    roll = lambda value, by: pltpu.roll(value, by, 0)

    def own(i, _):
        x = 2 * i + HALO
        first, second, third = from_low[i, 0], from_low[i, 1], from_low[i, 2]
        mixed = jnp.where(sub >= 6, roll(second, 6), roll(first, 3))
        v[x, 0:8] = jnp.where(low_keep, first, 0.0)
        v[x + 1, 0:8] = jnp.where(low_keep, second, 0.0)
        c[x, 0:8] = jnp.where(low_keep, third, 0.0)
        c[x + 1, 0:8] = jnp.where(low_keep, mixed, 0.0)
        phi[x, 0:8] = jnp.where(low_keep, roll(second, 5), 0.0)
        phi[x + 1, 0:8] = jnp.where(low_keep, roll(third, 5), 0.0)
        first, second, third = from_high[i, 0], from_high[i, 1], from_high[i, 2]
        mixed = jnp.where(sub < 3, roll(first, 3), roll(second, 6))
        v[x, 24:32] = jnp.where(high_keep, first, 0.0)
        v[x + 1, 24:32] = jnp.where(high_keep, second, 0.0)
        c[x, 24:32] = jnp.where(high_keep, third, 0.0)
        c[x + 1, 24:32] = jnp.where(high_keep, mixed, 0.0)
        phi[x, 24:32] = jnp.where(high_keep, roll(second, 1), 0.0)
        phi[x + 1, 24:32] = jnp.where(high_keep, roll(third, 1), 0.0)
        for k in range(2):
            v[x + k, 8:24] = guess[2 * i + k]
            phi[x + k, 8:24] = pot[2 * i + k]
            c[x + k, 8:24] = cond[2 * i + k]
        return 0

    lax.fori_loop(0, WX // 2, own, 0, unroll=2)
    blank = jnp.zeros((EY, DEPTH), f32)
    empty = jnp.where(gx == 0, 0, WX + HALO)
    there = jnp.where(gx == 0, WX + HALO, 0)
    for k in range(HALO):
        for ref in (v, phi, c):
            ref[empty + k] = blank
        for ref in (v, phi, c):
            ref[there + k] = blank
        v[there + k, 8:24] = across[k]
        c[there + k, 8:24] = across[HALO + k]
    phi[jnp.where(gx == 0, WX + HALO, HALO - 1), 8:24] = across[2 * HALO]
    count = spots.shape[0]
    before, after = jnp.maximum(gy - 1, 0), jnp.minimum(gy + 1, count - 1)
    for on, source, start, is_low in ((low_on, before, 0, True), (high_on, after, 24, False)):
        tiles = uncorner([spots[source, k] for k in range(3)], is_low)
        for (n, k), tile in tiles.items():
            x = jnp.where(gx == 0, WX + HALO + k - 1, HALO - k)
            (v, c)[n][x, start : start + 8] = jnp.where(on, tile, 0.0)

    lane = lax.broadcasted_iota(i32, (1, EY, DEPTH), 2)
    last, first = lane == DEPTH - 1, lane == 0
    fx[0] = 0.5 * (c[0] + c[1])

    def coefficients(i):
        here = c[i]
        after = 0.5 * (here + c[ahead(i)])
        before = 0.5 * (c[behind(i)] + here)
        side = 0.5 * (here + pltpu.roll(here, EY - 1, 1))
        deep = 0.5 * (here + jnp.where(last, 0.0, pltpu.roll(here, DEPTH - 1, 2)))
        back = jnp.where(first, 0.5 * here, pltpu.roll(deep, 1, 2))
        total = after + before + side + pltpu.roll(side, 1, 1) + deep + back
        fx[i] = after
        fy[i] = side
        fz[i] = jnp.where(last, 0.0, deep)
        diag[i] = total
        inv[i] = jnp.where(here > 0.0, 1.0 / total, 0.0)

    over_rows(1, EX - 1, coefficients)

    lx = rec[0:1, :] - gx * WX + HALO
    ly = rec[1:2, :] - gy * WY + 8
    near = (lx >= 0) & (lx < EX) & (ly >= 0) & (ly < EY)
    row = jnp.where(near, lx * EY + ly, -1)
    total = spots[0, 3]
    for k in range(1, count):
        total = total + spots[k, 3]
    anchor = total[4:5, :]
    pieces = [
        total[k : k + 1, :] - anchor - obs[:, DEPTH * k : DEPTH * (k + 1)]
        for k in range(NREC // DEPTH)
    ]
    misfit = jnp.concatenate(pieces, axis=1)
    whole = jnp.sum(misfit, axis=1, keepdims=True)
    level = lax.broadcasted_iota(i32, (DEPTH, NREC), 0) == rec[2:3, :]
    weights = jnp.concatenate(split3(jnp.where(level, misfit, 0.0)), axis=0)
    span = EX // SCATTERS
    for k in range(SCATTERS):
        ids = lax.broadcasted_iota(i32, (span * EY, NREC), 0) + k * span * EY
        hot = jnp.where(ids == row, 1.0, 0.0).astype(bf16)
        got = lax.dot_general(
            hot, weights, (((1,), (1,)), ((), ())), preferred_element_type=f32
        )
        placed = got[:, :DEPTH] + (got[:, DEPTH : 2 * DEPTH] + got[:, 2 * DEPTH :])
        r[k * span : (k + 1) * span] = placed.reshape(span, EY, DEPTH)

    ex = elec[0, 0] - gx * WX + HALO
    ey = elec[0, 1] - gy * WY + 8
    held = (ex >= 0) & (ex < EX) & (ey >= 0) & (ey < EY)
    cx = jnp.clip(ex, 0, EX - 1)
    spot = (
        (lax.broadcasted_iota(i32, (EY, DEPTH), 0) == ey)
        & (lax.broadcasted_iota(i32, (EY, DEPTH), 1) == elec[0, 2])
        & held
    )
    r[cx] = r[cx] - jnp.where(spot, whole, 0.0)

    def applied(ref, i):
        here = ref[i]
        out = diag[i] * here - fx[i] * ref[ahead(i)] - fx[behind(i)] * ref[behind(i)]
        side = fy[i]
        out = out - side * pltpu.roll(here, EY - 1, 1) - pltpu.roll(side * here, 1, 1)
        deep = fz[i]
        return out - deep * pltpu.roll(here, DEPTH - 1, 2) - pltpu.roll(deep * here, 1, 2)

    def begin(i):
        left = r[i] - applied(v, i)
        r[i] = left
        d0[i] = left * inv[i] * (1.0 / THETA)

    over_rows(1, EX - 1, begin)
    ratio = 1.0 / SIGMA
    source, target = d0, d1
    for sweep in range(SWEEPS - 1):
        following = 1.0 / (2.0 * SIGMA - ratio)
        keep, gain = following * ratio, 2.0 * following / DELTA

        def advance(i, source=source, target=target, keep=keep, gain=gain):
            here = source[i]
            left = r[i] - applied(source, i)
            new = v[i] + here
            v[i] = new
            r[i] = left
            target[i] = keep * here + gain * (left * inv[i])

        over_rows(2 + sweep, EX - 2 - sweep, advance)
        ratio = following
        source, target = target, source

    v[HALO - 1] = v[HALO - 1] + source[HALO - 1]
    v[WX + HALO] = v[WX + HALO] + source[WX + HALO]
    squares[...] = jnp.zeros((8, DEPTH), f32)

    def finish(i):
        here = source[i]
        left = r[i] - applied(source, i)
        new = v[i] + here
        v[i] = new
        final[shifted(i)] = new[:, 8:24]
        left = left[:, 8:24]
        left = left * left
        squares[...] += jnp.sum(left[:, :8] + left[:, 8:], axis=0)

    over_rows(HALO, WX + HALO, finish)
    store = pltpu.make_async_copy(final, adjoint, sem)
    store.start()

    def product(i):
        a, p = v[i], phi[i]
        out = (a - v[ahead(i)]) * (p - phi[ahead(i)]) + (a - v[behind(i)]) * (p - phi[behind(i)])
        side = (a - pltpu.roll(a, EY - 1, 1)) * (p - pltpu.roll(p, EY - 1, 1))
        out = out + side + pltpu.roll(side, 1, 1)
        deep = (a - jnp.where(last, 0.0, pltpu.roll(a, DEPTH - 1, 2))) * (
            p - jnp.where(last, 0.0, pltpu.roll(p, DEPTH - 1, 2))
        )
        out = out + deep + jnp.where(first, a * p, pltpu.roll(deep, 1, 2))
        term[shifted(i)] = -0.5 * out[:, 8:24]

    over_rows(HALO, WX + HALO, product)
    store.wait()


def plane_kernel(parts, own, got, out, acc):
    for q in range(LINE):
        total = parts[0, q]
        square = total * total
        for k in range(1, PLANE):
            more = parts[k, q]
            total = total + more
            square = square + more * more
        out[q, 0] = total
        out[q, 1] = square
    acc[...] = own[...] + got[...]


def scale_kernel(sources, parts, out):
    total, square = parts[0, 0], parts[0, 1]
    for q in range(1, LINE):
        total = total + parts[q, 0]
        square = square + parts[q, 1]
    value = total * lax.rsqrt(square / sources + 1.0)
    for q in range(LINE):
        out[q] = value


def spread_kernel(rows, own, got, out, acc):
    value = rows[...]
    for k in range(PLANE):
        out[k] = value
    acc[...] = own[...] + got[...]


def rms_kernel(cells, own, got, rms):
    total = jnp.sum(own[...] + got[...], axis=0, keepdims=True)
    rms[...] = jnp.broadcast_to(
        jnp.sqrt(jnp.sum(total, axis=1, keepdims=True) / cells), (1, DEPTH)
    )


VM = pl.BlockSpec(memory_space=pltpu.VMEM)
SM = pl.BlockSpec(memory_space=pltpu.SMEM)
HB = pl.BlockSpec(memory_space=pl.ANY)


def call(kernel, shapes, specs, *args, scratch=(), limit=48 * 1024 * 1024, outs=None):
    return pl.pallas_call(
        kernel,
        out_shape=[jax.ShapeDtypeStruct(shape, f32) for shape in shapes],
        in_specs=specs,
        out_specs=outs or [VM] * len(shapes),
        scratch_shapes=list(scratch),
        compiler_params=pltpu.CompilerParams(vmem_limit_bytes=limit),
    )(*args)


def body(conductivity, potential, adjoint_guess, observed, receiver_cells, electrodes):
    sources = lax.axis_size("src")
    pot, guess = potential[0], adjoint_guess[0]
    elec = jnp.transpose(electrodes)
    tile = (8, DEPTH)
    swap_x = [(0, 1), (1, 0)]
    (mine,) = call(
        gather_kernel, [(2 * HALO + 2, WY, DEPTH)], [SM, HB, HB, HB, HB],
        elec, receiver_cells, pot, guess, conductivity,
        scratch=[
            pltpu.VMEM((3, NREC), i32),
            pltpu.VMEM((WX, WY, DEPTH), f32),
            pltpu.SemaphoreType.DMA((3 + LOADS,)),
        ],
        limit=GRANT,
    )
    theirs = lax.ppermute(mine, "gx", swap_x)
    faces = (WX // 2, 3, 8, DEPTH)
    up, down, partial = call(
        pack_kernel, [faces, faces, tile], [HB] + [VM] * 3, mine, pot, guess, conductivity,
        scratch=[pltpu.SemaphoreType.DMA],
    )
    ring = lambda step: [(i, (i + step) % 4) for i in range(4)]
    from_low = lax.ppermute(up, "gy", ring(1))
    from_high = lax.ppermute(down, "gy", ring(3))
    (spots,) = call(
        corner_kernel, [(lax.axis_size("gy"), 4, 8, DEPTH)], [VM] * 2, partial, theirs
    )
    spots = lax.all_to_all(spots, "gy", 0, 0, tiled=True)
    block = (WX, WY, DEPTH)
    adjoint, term, squares = call(
        smooth_kernel, [block, block, tile], [VM, SM] + [VM] * 8,
        receiver_cells, elec, observed, pot, guess, conductivity,
        theirs, from_low, from_high, spots,
        scratch=[pltpu.VMEM((EX, EY, DEPTH), f32)] * 11
        + [pltpu.VMEM(block, f32), pltpu.SemaphoreType.DMA],
        outs=[HB, VM, VM],
    )
    planes = [[z * PLANE + k for k in range(PLANE)] for z in range(LINE)]
    lines = [[z * PLANE + k for z in range(LINE)] for k in range(PLANE)]

    def exchange(value, groups):
        return lax.all_to_all(value, "src", 0, 0, axis_index_groups=groups, tiled=True)

    other = lax.ppermute(squares, "gx", swap_x)
    got = exchange(term.reshape(PLANE, LINE, WY, DEPTH), planes)
    sums, squares = call(
        plane_kernel, [(LINE, 2, WY, DEPTH), tile], [VM] * 3, got, squares, other
    )
    got = exchange(sums, lines)
    (scaled,) = call(
        lambda *refs: scale_kernel(sources, *refs), [(LINE, WY, DEPTH)], [VM], got
    )
    other = lax.ppermute(squares, "gy", [(0, 1), (1, 0), (2, 3), (3, 2)])
    got = exchange(scaled, lines)
    spread, squares = call(
        spread_kernel, [(PLANE, LINE, WY, DEPTH), tile], [VM] * 3, got, squares, other
    )
    other = lax.ppermute(squares, "gy", [(0, 2), (2, 0), (1, 3), (3, 1)])
    gradient = exchange(spread, planes).reshape(block)
    cells = WX * lax.axis_size("gx") * WY * lax.axis_size("gy") * DEPTH
    (rms,) = call(
        lambda *refs: rms_kernel(cells, *refs), [(1, DEPTH)], [VM] * 2, squares, other
    )
    return adjoint[None], rms[0, :1], gradient


def solution(mesh):
    return jax.shard_map(
        body,
        mesh=mesh,
        in_specs=(
            P("gx", "gy", None),
            P("src", "gx", "gy", None),
            P("src", "gx", "gy", None),
            P("src", None),
            P(),
            P(None, "src"),
        ),
        out_specs=(P("src", "gx", "gy", None), P("src"), P("gx", "gy", None)),
        check_vma=False,
    )
```

```python
import jax
import jax.numpy as jnp
from jax import lax
from jax.experimental import pallas as pl
from jax.experimental.pallas import tpu as pltpu
from jax.sharding import PartitionSpec as P

SWEEPS = 4
LOW, HIGH = 0.25, 2.0
THETA = 0.5 * (HIGH + LOW)
DELTA = 0.5 * (HIGH - LOW)
SIGMA = THETA / DELTA

WX, WY, DEPTH = 64, 16, 128
NREC = 512
HALO = SWEEPS + 1
EX = WX + 2 * HALO
EY = WY + 16
LINE = 8
PLANE = 8
ROWS = 36
SCATTERS = 2
LOADS = 8
GRANT = 63_800_000
f32, bf16, i32 = jnp.float32, jnp.bfloat16, jnp.int32


def split3(value):
    top = value.astype(bf16)
    rest = value - top.astype(f32)
    middle = rest.astype(bf16)
    low = (rest - middle.astype(f32)).astype(bf16)
    return top, middle, low


def ahead(i):
    return pl.ds(i.start + 1, i.size)


def behind(i):
    return pl.ds(i.start - 1, i.size)


def shifted(i):
    return pl.ds(i.start - HALO, i.size)


def over_rows(low, high, step):
    count, rest = divmod(high - low, ROWS)

    def turn(k, _):
        step(pl.ds(low + k * ROWS, ROWS))
        return 0

    lax.fori_loop(0, count, turn, 0)
    if rest:
        step(pl.ds(high - rest, rest))


def sides(gy):
    return gy > 0, gy < lax.axis_size("gy") - 1


def corner(near, low):
    sub = lax.broadcasted_iota(i32, (8, DEPTH), 0)
    tiles = []
    for n in range(2):
        if low:
            second = jnp.where(sub == 0, pltpu.roll(near(n, 4), 1, 0), pltpu.roll(near(n, 2), 4, 0))
            tiles.append(jnp.where(sub >= 4, near(n, 1), second))
        else:
            second = jnp.where(sub == 7, pltpu.roll(near(n, 4), 7, 0), pltpu.roll(near(n, 2), 4, 0))
            tiles.append(jnp.where(sub < 4, near(n, 1), second))
    if low:
        tiles.append(jnp.where(sub >= 6, near(0, 3), pltpu.roll(near(1, 3), 6, 0)))
    else:
        tiles.append(jnp.where(sub < 2, near(0, 3), pltpu.roll(near(1, 3), 2, 0)))
    return tiles


def uncorner(tiles, low):
    sub = lax.broadcasted_iota(i32, (8, DEPTH), 0)
    out = {}
    for n in range(2):
        if low:
            out[n, 1] = jnp.where(sub >= 4, tiles[n], 0.0)
            out[n, 2] = jnp.where(sub >= 5, pltpu.roll(tiles[n], 4, 0), 0.0)
            out[n, 3] = jnp.where(sub >= 6, pltpu.roll(tiles[2], 2 * n, 0) if n else tiles[2], 0.0)
            out[n, 4] = jnp.where(sub == 7, pltpu.roll(tiles[n], 7, 0), 0.0)
        else:
            out[n, 1] = jnp.where(sub < 4, tiles[n], 0.0)
            out[n, 2] = jnp.where(sub < 3, pltpu.roll(tiles[n], 4, 0), 0.0)
            out[n, 3] = jnp.where(sub < 2, pltpu.roll(tiles[2], 6, 0) if n else tiles[2], 0.0)
            out[n, 4] = jnp.where(sub == 0, pltpu.roll(tiles[n], 1, 0), 0.0)
    return out


def gather_kernel(elec_in, rec_in, pot_in, guess, cond, out, elec, rec, pot, sems):
    gx, gy = lax.axis_index("gx"), lax.axis_index("gy")
    base = jnp.where(gx == 0, WX - HALO, 0)
    step = WX // LOADS
    pairs = [(rec_in, rec), (elec_in, elec)]
    for k in range(LOADS):
        pairs.append((pot_in.at[pl.ds(k * step, step)], pot.at[pl.ds(k * step, step)]))
    pairs.append((guess.at[pl.ds(base, HALO)], out.at[pl.ds(0, HALO)]))
    pairs.append((cond.at[pl.ds(base, HALO)], out.at[pl.ds(HALO, HALO)]))
    loads = [
        pltpu.make_async_copy(source, target, sems.at[k])
        for k, (source, target) in enumerate(pairs)
    ]
    for load in loads:
        load.start()
    loads[0].wait()
    lx = rec[0:1, :] - gx * WX
    ly = rec[1:2, :] - gy * WY
    inside = (lx >= 0) & (lx < WX) & (ly >= 0) & (ly < WY)
    row = jnp.where(inside, lx * WY + ly, -1)
    hot = jnp.where(lax.broadcasted_iota(i32, (WX * WY, NREC), 0) == row, 1.0, 0.0).astype(bf16)
    for load in loads[1:]:
        load.wait()
    turned = jnp.transpose(pot[...].reshape(WX * WY, DEPTH))
    parts = [jnp.dot(part, hot, preferred_element_type=f32) for part in split3(turned)]
    values = parts[0] + (parts[1] + parts[2])
    level = lax.broadcasted_iota(i32, (DEPTH, NREC), 0) == rec[2:3, :]
    picked = jnp.sum(jnp.where(level, values, 0.0), axis=0, keepdims=True)
    for k in range(NREC // DEPTH):
        out[2 * HALO + 1, k : k + 1, :] = picked[:, DEPTH * k : DEPTH * (k + 1)]
    ex = elec[0, 0] - gx * WX
    ey = elec[0, 1] - gy * WY
    held = (ex >= 0) & (ex < WX) & (ey >= 0) & (ey < WY)
    cx = jnp.clip(ex, 0, WX - 1)
    cy = jnp.clip(ey, 0, WY - 1)
    plane = pot[cx]
    here = (lax.broadcasted_iota(i32, (WY, DEPTH), 0) == cy) & (
        lax.broadcasted_iota(i32, (WY, DEPTH), 1) == elec[0, 2]
    )
    there = jnp.sum(jnp.where(here & held, plane, 0.0), axis=0, keepdims=True)
    value = jnp.sum(there, axis=1, keepdims=True)
    out[2 * HALO + 1, 4:5, :] = jnp.broadcast_to(value, (1, DEPTH))
    out[2 * HALO + 1, 5:16, :] = jnp.zeros((11, DEPTH), f32)
    out[2 * HALO] = pot[jnp.where(gx == 0, WX - 1, 0)]


def pack_kernel(mine, pot, guess, cond, up, down, partial, sem):
    load = pltpu.make_async_copy(mine.at[2 * HALO + 1, pl.ds(0, 8)], partial, sem)
    load.start()
    sub = lax.broadcasted_iota(i32, (1, 8, DEPTH), 1)
    for out, span, keep, turn in ((up, slice(8, 16), sub >= 3, 3), (down, slice(0, 8), sub < 5, 7)):
        g, p, c = (ref[:, span].reshape(WX // 2, 2, 8, DEPTH) for ref in (guess, pot, cond))
        at_pot = sub == (2 if turn == 3 else 7)
        roll = lambda value, by: pltpu.roll(value, by, 1)
        rest = jnp.where(at_pot, roll(p[:, 0], turn), roll(c[:, 1], 2))
        out[:, 0] = jnp.where(keep, g[:, 0], roll(c[:, 1], 5))
        out[:, 1] = jnp.where(keep, g[:, 1], rest)
        out[:, 2] = jnp.where(keep, c[:, 0], roll(p[:, 1], turn))
    load.wait()


def corner_kernel(own, theirs, spots):
    gx, gy = lax.axis_index("gx"), lax.axis_index("gy")

    def near(half):
        def tile(n, k):
            x = n * HALO + jnp.where(gx == 0, k - 1, HALO - k)
            return theirs[x, 8 * half : 8 * half + 8]

        return tile

    count = spots.shape[0]
    total = own[...] + theirs[2 * HALO + 1, 0:8]
    high, low = corner(near(1), True), corner(near(0), False)
    for j in range(count):
        for k in range(3):
            spots[j, k] = jnp.where(j > gy, high[k], low[k])
        spots[j, 3] = total


def smooth_kernel(
    rec, elec, obs, pot, guess, cond, across, from_low, from_high, spots,
    adjoint, term, squares,
    c, v, r, d0, d1, fx, fy, fz, diag, inv, phi, final, sem,
):
    gx, gy = lax.axis_index("gx"), lax.axis_index("gy")
    sub = lax.broadcasted_iota(i32, (8, DEPTH), 0)
    low_on, high_on = (gy > 0), (gy < lax.axis_size("gy") - 1)
    low_keep, high_keep = low_on & (sub >= 3), high_on & (sub < 5)
    roll = lambda value, by: pltpu.roll(value, by, 0)

    def own(i, _):
        x = 2 * i + HALO
        first, second, third = from_low[i, 0], from_low[i, 1], from_low[i, 2]
        mixed = jnp.where(sub >= 6, roll(second, 6), roll(first, 3))
        v[x, 0:8] = jnp.where(low_keep, first, 0.0)
        v[x + 1, 0:8] = jnp.where(low_keep, second, 0.0)
        c[x, 0:8] = jnp.where(low_keep, third, 0.0)
        c[x + 1, 0:8] = jnp.where(low_keep, mixed, 0.0)
        phi[x, 0:8] = jnp.where(low_keep, roll(second, 5), 0.0)
        phi[x + 1, 0:8] = jnp.where(low_keep, roll(third, 5), 0.0)
        first, second, third = from_high[i, 0], from_high[i, 1], from_high[i, 2]
        mixed = jnp.where(sub < 3, roll(first, 3), roll(second, 6))
        v[x, 24:32] = jnp.where(high_keep, first, 0.0)
        v[x + 1, 24:32] = jnp.where(high_keep, second, 0.0)
        c[x, 24:32] = jnp.where(high_keep, third, 0.0)
        c[x + 1, 24:32] = jnp.where(high_keep, mixed, 0.0)
        phi[x, 24:32] = jnp.where(high_keep, roll(second, 1), 0.0)
        phi[x + 1, 24:32] = jnp.where(high_keep, roll(third, 1), 0.0)
        for k in range(2):
            v[x + k, 8:24] = guess[2 * i + k]
            phi[x + k, 8:24] = pot[2 * i + k]
            c[x + k, 8:24] = cond[2 * i + k]
        return 0

    lax.fori_loop(0, WX // 2, own, 0, unroll=2)
    blank = jnp.zeros((EY, DEPTH), f32)
    empty = jnp.where(gx == 0, 0, WX + HALO)
    there = jnp.where(gx == 0, WX + HALO, 0)
    for k in range(HALO):
        for ref in (v, phi, c):
            ref[empty + k] = blank
        for ref in (v, phi, c):
            ref[there + k] = blank
        v[there + k, 8:24] = across[k]
        c[there + k, 8:24] = across[HALO + k]
    phi[jnp.where(gx == 0, WX + HALO, HALO - 1), 8:24] = across[2 * HALO]
    count = spots.shape[0]
    before, after = jnp.maximum(gy - 1, 0), jnp.minimum(gy + 1, count - 1)
    for on, source, start, is_low in ((low_on, before, 0, True), (high_on, after, 24, False)):
        tiles = uncorner([spots[source, k] for k in range(3)], is_low)
        for (n, k), tile in tiles.items():
            x = jnp.where(gx == 0, WX + HALO + k - 1, HALO - k)
            (v, c)[n][x, start : start + 8] = jnp.where(on, tile, 0.0)

    lane = lax.broadcasted_iota(i32, (1, EY, DEPTH), 2)
    last, first = lane == DEPTH - 1, lane == 0
    fx[0] = 0.5 * (c[0] + c[1])

    def coefficients(i):
        here = c[i]
        after = 0.5 * (here + c[ahead(i)])
        before = 0.5 * (c[behind(i)] + here)
        side = 0.5 * (here + pltpu.roll(here, EY - 1, 1))
        deep = 0.5 * (here + jnp.where(last, 0.0, pltpu.roll(here, DEPTH - 1, 2)))
        back = jnp.where(first, 0.5 * here, pltpu.roll(deep, 1, 2))
        total = after + before + side + pltpu.roll(side, 1, 1) + deep + back
        fx[i] = after
        fy[i] = side
        fz[i] = jnp.where(last, 0.0, deep)
        diag[i] = total
        inv[i] = jnp.where(here > 0.0, 1.0 / total, 0.0)

    over_rows(1, EX - 1, coefficients)

    lx = rec[0:1, :] - gx * WX + HALO
    ly = rec[1:2, :] - gy * WY + 8
    near = (lx >= 0) & (lx < EX) & (ly >= 0) & (ly < EY)
    row = jnp.where(near, lx * EY + ly, -1)
    total = spots[0, 3]
    for k in range(1, count):
        total = total + spots[k, 3]
    anchor = total[4:5, :]
    pieces = [
        total[k : k + 1, :] - anchor - obs[:, DEPTH * k : DEPTH * (k + 1)]
        for k in range(NREC // DEPTH)
    ]
    misfit = jnp.concatenate(pieces, axis=1)
    whole = jnp.sum(misfit, axis=1, keepdims=True)
    level = lax.broadcasted_iota(i32, (DEPTH, NREC), 0) == rec[2:3, :]
    weights = jnp.concatenate(split3(jnp.where(level, misfit, 0.0)), axis=0)
    span = EX // SCATTERS
    for k in range(SCATTERS):
        ids = lax.broadcasted_iota(i32, (span * EY, NREC), 0) + k * span * EY
        hot = jnp.where(ids == row, 1.0, 0.0).astype(bf16)
        got = lax.dot_general(
            hot, weights, (((1,), (1,)), ((), ())), preferred_element_type=f32
        )
        placed = got[:, :DEPTH] + (got[:, DEPTH : 2 * DEPTH] + got[:, 2 * DEPTH :])
        r[k * span : (k + 1) * span] = placed.reshape(span, EY, DEPTH)

    ex = elec[0, 0] - gx * WX + HALO
    ey = elec[0, 1] - gy * WY + 8
    held = (ex >= 0) & (ex < EX) & (ey >= 0) & (ey < EY)
    cx = jnp.clip(ex, 0, EX - 1)
    spot = (
        (lax.broadcasted_iota(i32, (EY, DEPTH), 0) == ey)
        & (lax.broadcasted_iota(i32, (EY, DEPTH), 1) == elec[0, 2])
        & held
    )
    r[cx] = r[cx] - jnp.where(spot, whole, 0.0)

    def applied(ref, i):
        here = ref[i]
        out = diag[i] * here - fx[i] * ref[ahead(i)] - fx[behind(i)] * ref[behind(i)]
        side = fy[i]
        out = out - side * pltpu.roll(here, EY - 1, 1) - pltpu.roll(side * here, 1, 1)
        deep = fz[i]
        return out - deep * pltpu.roll(here, DEPTH - 1, 2) - pltpu.roll(deep * here, 1, 2)

    def begin(i):
        left = r[i] - applied(v, i)
        r[i] = left
        d0[i] = left * inv[i] * (1.0 / THETA)

    over_rows(1, EX - 1, begin)
    ratio = 1.0 / SIGMA
    source, target = d0, d1
    for sweep in range(SWEEPS - 1):
        following = 1.0 / (2.0 * SIGMA - ratio)
        keep, gain = following * ratio, 2.0 * following / DELTA

        def advance(i, source=source, target=target, keep=keep, gain=gain):
            here = source[i]
            left = r[i] - applied(source, i)
            new = v[i] + here
            v[i] = new
            r[i] = left
            target[i] = keep * here + gain * (left * inv[i])

        over_rows(2 + sweep, EX - 2 - sweep, advance)
        ratio = following
        source, target = target, source

    v[HALO - 1] = v[HALO - 1] + source[HALO - 1]
    v[WX + HALO] = v[WX + HALO] + source[WX + HALO]
    squares[...] = jnp.zeros((8, DEPTH), f32)

    def finish(i):
        here = source[i]
        left = r[i] - applied(source, i)
        new = v[i] + here
        v[i] = new
        final[shifted(i)] = new[:, 8:24]
        left = left[:, 8:24]
        left = left * left
        squares[...] += jnp.sum(left[:, :8] + left[:, 8:], axis=0)

    over_rows(HALO, WX + HALO, finish)
    store = pltpu.make_async_copy(final, adjoint, sem)
    store.start()

    def product(i):
        a, p = v[i], phi[i]
        out = (a - v[ahead(i)]) * (p - phi[ahead(i)]) + (a - v[behind(i)]) * (p - phi[behind(i)])
        side = (a - pltpu.roll(a, EY - 1, 1)) * (p - pltpu.roll(p, EY - 1, 1))
        out = out + side + pltpu.roll(side, 1, 1)
        deep = (a - jnp.where(last, 0.0, pltpu.roll(a, DEPTH - 1, 2))) * (
            p - jnp.where(last, 0.0, pltpu.roll(p, DEPTH - 1, 2))
        )
        out = out + deep + jnp.where(first, a * p, pltpu.roll(deep, 1, 2))
        term[shifted(i)] = -0.5 * out[:, 8:24]

    over_rows(HALO, WX + HALO, product)
    store.wait()


def plane_kernel(parts, own, got, out, acc):
    for q in range(LINE):
        total = parts[0, q]
        square = total * total
        for k in range(1, PLANE):
            more = parts[k, q]
            total = total + more
            square = square + more * more
        out[q, 0] = total
        out[q, 1] = square
    acc[...] = own[...] + got[...]


def scale_kernel(sources, parts, out):
    total, square = parts[0, 0], parts[0, 1]
    for q in range(1, LINE):
        total = total + parts[q, 0]
        square = square + parts[q, 1]
    value = total * lax.rsqrt(square / sources + 1.0)
    for q in range(LINE):
        out[q] = value


def spread_kernel(rows, own, got, out, acc):
    value = rows[...]
    for k in range(PLANE):
        out[k] = value
    acc[...] = own[...] + got[...]


def rms_kernel(cells, own, got, rms):
    total = jnp.sum(own[...] + got[...], axis=0, keepdims=True)
    rms[...] = jnp.broadcast_to(
        jnp.sqrt(jnp.sum(total, axis=1, keepdims=True) / cells), (1, DEPTH)
    )


VM = pl.BlockSpec(memory_space=pltpu.VMEM)
SM = pl.BlockSpec(memory_space=pltpu.SMEM)
HB = pl.BlockSpec(memory_space=pl.ANY)


def call(kernel, shapes, specs, *args, scratch=(), limit=48 * 1024 * 1024, outs=None):
    return pl.pallas_call(
        kernel,
        out_shape=[jax.ShapeDtypeStruct(shape, f32) for shape in shapes],
        in_specs=specs,
        out_specs=outs or [VM] * len(shapes),
        scratch_shapes=list(scratch),
        compiler_params=pltpu.CompilerParams(vmem_limit_bytes=limit),
    )(*args)


def body(conductivity, potential, adjoint_guess, observed, receiver_cells, electrodes):
    sources = lax.axis_size("src")
    pot, guess = potential[0], adjoint_guess[0]
    elec = jnp.transpose(electrodes)
    tile = (8, DEPTH)
    swap_x = [(0, 1), (1, 0)]
    (mine,) = call(
        gather_kernel, [(2 * HALO + 2, WY, DEPTH)], [HB] * 5,
        elec, receiver_cells, pot, guess, conductivity,
        scratch=[
            pltpu.SMEM((1, 3), i32),
            pltpu.VMEM((3, NREC), i32),
            pltpu.VMEM((WX, WY, DEPTH), f32),
            pltpu.SemaphoreType.DMA((4 + LOADS,)),
        ],
        limit=GRANT,
    )
    theirs = lax.ppermute(mine, "gx", swap_x)
    faces = (WX // 2, 3, 8, DEPTH)
    up, down, partial = call(
        pack_kernel, [faces, faces, tile], [HB] + [VM] * 3, mine, pot, guess, conductivity,
        scratch=[pltpu.SemaphoreType.DMA],
    )
    ring = lambda step: [(i, (i + step) % 4) for i in range(4)]
    from_low = lax.ppermute(up, "gy", ring(1))
    from_high = lax.ppermute(down, "gy", ring(3))
    (spots,) = call(
        corner_kernel, [(lax.axis_size("gy"), 4, 8, DEPTH)], [VM] * 2, partial, theirs
    )
    spots = lax.all_to_all(spots, "gy", 0, 0, tiled=True)
    block = (WX, WY, DEPTH)
    adjoint, term, squares = call(
        smooth_kernel, [block, block, tile], [VM, SM] + [VM] * 8,
        receiver_cells, elec, observed, pot, guess, conductivity,
        theirs, from_low, from_high, spots,
        scratch=[pltpu.VMEM((EX, EY, DEPTH), f32)] * 11
        + [pltpu.VMEM(block, f32), pltpu.SemaphoreType.DMA],
        outs=[HB, VM, VM],
    )
    planes = [[z * PLANE + k for k in range(PLANE)] for z in range(LINE)]
    lines = [[z * PLANE + k for z in range(LINE)] for k in range(PLANE)]

    def exchange(value, groups):
        return lax.all_to_all(value, "src", 0, 0, axis_index_groups=groups, tiled=True)

    other = lax.ppermute(squares, "gx", swap_x)
    got = exchange(term.reshape(PLANE, LINE, WY, DEPTH), planes)
    sums, squares = call(
        plane_kernel, [(LINE, 2, WY, DEPTH), tile], [VM] * 3, got, squares, other
    )
    got = exchange(sums, lines)
    (scaled,) = call(
        lambda *refs: scale_kernel(sources, *refs), [(LINE, WY, DEPTH)], [VM], got
    )
    other = lax.ppermute(squares, "gy", [(0, 1), (1, 0), (2, 3), (3, 2)])
    got = exchange(scaled, lines)
    spread, squares = call(
        spread_kernel, [(PLANE, LINE, WY, DEPTH), tile], [VM] * 3, got, squares, other
    )
    other = lax.ppermute(squares, "gy", [(0, 2), (2, 0), (1, 3), (3, 1)])
    gradient = exchange(spread, planes).reshape(block)
    cells = WX * lax.axis_size("gx") * WY * lax.axis_size("gy") * DEPTH
    (rms,) = call(
        lambda *refs: rms_kernel(cells, *refs), [(1, DEPTH)], [VM] * 2, squares, other
    )
    return adjoint[None], rms[0, :1], gradient


def solution(mesh):
    return jax.shard_map(
        body,
        mesh=mesh,
        in_specs=(
            P("gx", "gy", None),
            P("src", "gx", "gy", None),
            P("src", "gx", "gy", None),
            P("src", None),
            P(),
            P(None, "src"),
        ),
        out_specs=(P("src", "gx", "gy", None), P("src"), P("gx", "gy", None)),
        check_vma=False,
    )
```

```python
import jax
import jax.numpy as jnp
from jax import lax
from jax.experimental import pallas as pl
from jax.experimental.pallas import tpu as pltpu
from jax.sharding import PartitionSpec as P

SWEEPS = 4
LOW, HIGH = 0.25, 2.0
THETA = 0.5 * (HIGH + LOW)
DELTA = 0.5 * (HIGH - LOW)
SIGMA = THETA / DELTA

WX, WY, DEPTH = 64, 16, 128
NREC = 512
HALO = SWEEPS + 1
EX = WX + 2 * HALO
EY = WY + 16
LINE = 8
PLANE = 8
ROWS = 36
SCATTERS = 2
LOADS = 8
GRANT = 63_800_000
f32, bf16, i32 = jnp.float32, jnp.bfloat16, jnp.int32


def split3(value):
    top = value.astype(bf16)
    rest = value - top.astype(f32)
    middle = rest.astype(bf16)
    low = (rest - middle.astype(f32)).astype(bf16)
    return top, middle, low


def ahead(i):
    return pl.ds(i.start + 1, i.size)


def behind(i):
    return pl.ds(i.start - 1, i.size)


def shifted(i):
    return pl.ds(i.start - HALO, i.size)


def over_rows(low, high, step):
    count, rest = divmod(high - low, ROWS)

    def turn(k, _):
        step(pl.ds(low + k * ROWS, ROWS))
        return 0

    lax.fori_loop(0, count, turn, 0)
    if rest:
        step(pl.ds(high - rest, rest))


def sides(gy):
    return gy > 0, gy < lax.axis_size("gy") - 1


def corner(near, low):
    sub = lax.broadcasted_iota(i32, (8, DEPTH), 0)
    tiles = []
    for n in range(2):
        if low:
            second = jnp.where(sub == 0, pltpu.roll(near(n, 4), 1, 0), pltpu.roll(near(n, 2), 4, 0))
            tiles.append(jnp.where(sub >= 4, near(n, 1), second))
        else:
            second = jnp.where(sub == 7, pltpu.roll(near(n, 4), 7, 0), pltpu.roll(near(n, 2), 4, 0))
            tiles.append(jnp.where(sub < 4, near(n, 1), second))
    if low:
        tiles.append(jnp.where(sub >= 6, near(0, 3), pltpu.roll(near(1, 3), 6, 0)))
    else:
        tiles.append(jnp.where(sub < 2, near(0, 3), pltpu.roll(near(1, 3), 2, 0)))
    return tiles


def uncorner(tiles, low):
    sub = lax.broadcasted_iota(i32, (8, DEPTH), 0)
    out = {}
    for n in range(2):
        if low:
            out[n, 1] = jnp.where(sub >= 4, tiles[n], 0.0)
            out[n, 2] = jnp.where(sub >= 5, pltpu.roll(tiles[n], 4, 0), 0.0)
            out[n, 3] = jnp.where(sub >= 6, pltpu.roll(tiles[2], 2 * n, 0) if n else tiles[2], 0.0)
            out[n, 4] = jnp.where(sub == 7, pltpu.roll(tiles[n], 7, 0), 0.0)
        else:
            out[n, 1] = jnp.where(sub < 4, tiles[n], 0.0)
            out[n, 2] = jnp.where(sub < 3, pltpu.roll(tiles[n], 4, 0), 0.0)
            out[n, 3] = jnp.where(sub < 2, pltpu.roll(tiles[2], 6, 0) if n else tiles[2], 0.0)
            out[n, 4] = jnp.where(sub == 0, pltpu.roll(tiles[n], 1, 0), 0.0)
    return out


def gather_kernel(elec_in, rec_in, pot_in, guess, cond, out, elec, rec, pot, sems):
    gx, gy = lax.axis_index("gx"), lax.axis_index("gy")
    base = jnp.where(gx == 0, WX - HALO, 0)
    step = WX // LOADS
    pairs = [(rec_in, rec), (elec_in, elec)]
    for k in range(LOADS):
        pairs.append((pot_in.at[pl.ds(k * step, step)], pot.at[pl.ds(k * step, step)]))
    pairs.append((guess.at[pl.ds(base, HALO)], out.at[pl.ds(0, HALO)]))
    pairs.append((cond.at[pl.ds(base, HALO)], out.at[pl.ds(HALO, HALO)]))
    loads = [
        pltpu.make_async_copy(source, target, sems.at[k])
        for k, (source, target) in enumerate(pairs)
    ]
    for load in loads:
        load.start()
    loads[0].wait()
    lx = rec[0:1, :] - gx * WX
    ly = rec[1:2, :] - gy * WY
    inside = (lx >= 0) & (lx < WX) & (ly >= 0) & (ly < WY)
    row = jnp.where(inside, lx * WY + ly, -1)
    hot = jnp.where(lax.broadcasted_iota(i32, (WX * WY, NREC), 0) == row, 1.0, 0.0).astype(bf16)
    for load in loads[1:]:
        load.wait()
    turned = jnp.transpose(pot[...].reshape(WX * WY, DEPTH))
    parts = [jnp.dot(part, hot, preferred_element_type=f32) for part in split3(turned)]
    values = parts[0] + (parts[1] + parts[2])
    level = lax.broadcasted_iota(i32, (DEPTH, NREC), 0) == rec[2:3, :]
    picked = jnp.sum(jnp.where(level, values, 0.0), axis=0, keepdims=True)
    for k in range(NREC // DEPTH):
        out[2 * HALO + 1, k : k + 1, :] = picked[:, DEPTH * k : DEPTH * (k + 1)]
    ex = elec[0, 0] - gx * WX
    ey = elec[0, 1] - gy * WY
    held = (ex >= 0) & (ex < WX) & (ey >= 0) & (ey < WY)
    cx = jnp.clip(ex, 0, WX - 1)
    cy = jnp.clip(ey, 0, WY - 1)
    plane = pot[cx]
    here = (lax.broadcasted_iota(i32, (WY, DEPTH), 0) == cy) & (
        lax.broadcasted_iota(i32, (WY, DEPTH), 1) == elec[0, 2]
    )
    there = jnp.sum(jnp.where(here & held, plane, 0.0), axis=0, keepdims=True)
    value = jnp.sum(there, axis=1, keepdims=True)
    out[2 * HALO + 1, 4:5, :] = jnp.broadcast_to(value, (1, DEPTH))
    out[2 * HALO + 1, 5:16, :] = jnp.zeros((11, DEPTH), f32)
    out[2 * HALO] = pot[jnp.where(gx == 0, WX - 1, 0)]


def pack_kernel(mine, pot, guess, cond, up, down, partial, sem):
    load = pltpu.make_async_copy(mine.at[2 * HALO + 1, pl.ds(0, 8)], partial, sem)
    load.start()
    sub = lax.broadcasted_iota(i32, (1, 8, DEPTH), 1)
    for out, span, keep, turn in ((up, slice(8, 16), sub >= 3, 3), (down, slice(0, 8), sub < 5, 7)):
        g, p, c = (ref[:, span].reshape(WX // 2, 2, 8, DEPTH) for ref in (guess, pot, cond))
        at_pot = sub == (2 if turn == 3 else 7)
        roll = lambda value, by: pltpu.roll(value, by, 1)
        rest = jnp.where(at_pot, roll(p[:, 0], turn), roll(c[:, 1], 2))
        out[:, 0] = jnp.where(keep, g[:, 0], roll(c[:, 1], 5))
        out[:, 1] = jnp.where(keep, g[:, 1], rest)
        out[:, 2] = jnp.where(keep, c[:, 0], roll(p[:, 1], turn))
    load.wait()


def corner_kernel(own, theirs, spots):
    gx, gy = lax.axis_index("gx"), lax.axis_index("gy")

    def near(half):
        def tile(n, k):
            x = n * HALO + jnp.where(gx == 0, k - 1, HALO - k)
            return theirs[x, 8 * half : 8 * half + 8]

        return tile

    count = spots.shape[0]
    total = own[...] + theirs[2 * HALO + 1, 0:8]
    high, low = corner(near(1), True), corner(near(0), False)
    for j in range(count):
        for k in range(3):
            spots[j, k] = jnp.where(j > gy, high[k], low[k])
        spots[j, 3] = total


def smooth_kernel(
    rec, elec, obs, pot, guess, cond, across, from_low, from_high, spots,
    adjoint, term, squares,
    c, v, r, d0, d1, fx, fy, fz, diag, inv, phi, final, sem,
):
    gx, gy = lax.axis_index("gx"), lax.axis_index("gy")
    sub = lax.broadcasted_iota(i32, (8, DEPTH), 0)
    low_on, high_on = (gy > 0), (gy < lax.axis_size("gy") - 1)
    low_keep, high_keep = low_on & (sub >= 3), high_on & (sub < 5)
    roll = lambda value, by: pltpu.roll(value, by, 0)

    def own(i, _):
        x = 2 * i + HALO
        first, second, third = from_low[i, 0], from_low[i, 1], from_low[i, 2]
        mixed = jnp.where(sub >= 6, roll(second, 6), roll(first, 3))
        v[x, 0:8] = jnp.where(low_keep, first, 0.0)
        v[x + 1, 0:8] = jnp.where(low_keep, second, 0.0)
        c[x, 0:8] = jnp.where(low_keep, third, 0.0)
        c[x + 1, 0:8] = jnp.where(low_keep, mixed, 0.0)
        phi[x, 0:8] = jnp.where(low_keep, roll(second, 5), 0.0)
        phi[x + 1, 0:8] = jnp.where(low_keep, roll(third, 5), 0.0)
        first, second, third = from_high[i, 0], from_high[i, 1], from_high[i, 2]
        mixed = jnp.where(sub < 3, roll(first, 3), roll(second, 6))
        v[x, 24:32] = jnp.where(high_keep, first, 0.0)
        v[x + 1, 24:32] = jnp.where(high_keep, second, 0.0)
        c[x, 24:32] = jnp.where(high_keep, third, 0.0)
        c[x + 1, 24:32] = jnp.where(high_keep, mixed, 0.0)
        phi[x, 24:32] = jnp.where(high_keep, roll(second, 1), 0.0)
        phi[x + 1, 24:32] = jnp.where(high_keep, roll(third, 1), 0.0)
        for k in range(2):
            v[x + k, 8:24] = guess[2 * i + k]
            phi[x + k, 8:24] = pot[2 * i + k]
            c[x + k, 8:24] = cond[2 * i + k]
        return 0

    lax.fori_loop(0, WX // 2, own, 0, unroll=2)
    blank = jnp.zeros((EY, DEPTH), f32)
    empty = jnp.where(gx == 0, 0, WX + HALO)
    there = jnp.where(gx == 0, WX + HALO, 0)
    for k in range(HALO):
        for ref in (v, phi, c):
            ref[empty + k] = blank
        for ref in (v, phi, c):
            ref[there + k] = blank
        v[there + k, 8:24] = across[k]
        c[there + k, 8:24] = across[HALO + k]
    phi[jnp.where(gx == 0, WX + HALO, HALO - 1), 8:24] = across[2 * HALO]
    count = spots.shape[0]
    before, after = jnp.maximum(gy - 1, 0), jnp.minimum(gy + 1, count - 1)
    for on, source, start, is_low in ((low_on, before, 0, True), (high_on, after, 24, False)):
        tiles = uncorner([spots[source, k] for k in range(3)], is_low)
        for (n, k), tile in tiles.items():
            x = jnp.where(gx == 0, WX + HALO + k - 1, HALO - k)
            (v, c)[n][x, start : start + 8] = jnp.where(on, tile, 0.0)

    lane = lax.broadcasted_iota(i32, (1, EY, DEPTH), 2)
    last, first = lane == DEPTH - 1, lane == 0
    fx[0] = 0.5 * (c[0] + c[1])

    def coefficients(i):
        here = c[i]
        after = 0.5 * (here + c[ahead(i)])
        before = 0.5 * (c[behind(i)] + here)
        side = 0.5 * (here + pltpu.roll(here, EY - 1, 1))
        deep = 0.5 * (here + jnp.where(last, 0.0, pltpu.roll(here, DEPTH - 1, 2)))
        back = jnp.where(first, 0.5 * here, pltpu.roll(deep, 1, 2))
        total = after + before + side + pltpu.roll(side, 1, 1) + deep + back
        fx[i] = after
        fy[i] = side
        fz[i] = jnp.where(last, 0.0, deep)
        diag[i] = total
        inv[i] = jnp.where(here > 0.0, 1.0 / total, 0.0)

    over_rows(1, EX - 1, coefficients)

    lx = rec[0:1, :] - gx * WX + HALO
    ly = rec[1:2, :] - gy * WY + 8
    near = (lx >= 0) & (lx < EX) & (ly >= 0) & (ly < EY)
    row = jnp.where(near, lx * EY + ly, -1)
    total = spots[0, 3]
    for k in range(1, count):
        total = total + spots[k, 3]
    anchor = total[4:5, :]
    pieces = [
        total[k : k + 1, :] - anchor - obs[:, DEPTH * k : DEPTH * (k + 1)]
        for k in range(NREC // DEPTH)
    ]
    misfit = jnp.concatenate(pieces, axis=1)
    whole = jnp.sum(misfit, axis=1, keepdims=True)
    level = lax.broadcasted_iota(i32, (DEPTH, NREC), 0) == rec[2:3, :]
    weights = jnp.concatenate(split3(jnp.where(level, misfit, 0.0)), axis=0)
    span = EX // SCATTERS
    for k in range(SCATTERS):
        ids = lax.broadcasted_iota(i32, (span * EY, NREC), 0) + k * span * EY
        hot = jnp.where(ids == row, 1.0, 0.0).astype(bf16)
        got = lax.dot_general(
            hot, weights, (((1,), (1,)), ((), ())), preferred_element_type=f32
        )
        placed = got[:, :DEPTH] + (got[:, DEPTH : 2 * DEPTH] + got[:, 2 * DEPTH :])
        r[k * span : (k + 1) * span] = placed.reshape(span, EY, DEPTH)

    ex = elec[0, 0] - gx * WX + HALO
    ey = elec[0, 1] - gy * WY + 8
    held = (ex >= 0) & (ex < EX) & (ey >= 0) & (ey < EY)
    cx = jnp.clip(ex, 0, EX - 1)
    spot = (
        (lax.broadcasted_iota(i32, (EY, DEPTH), 0) == ey)
        & (lax.broadcasted_iota(i32, (EY, DEPTH), 1) == elec[0, 2])
        & held
    )
    r[cx] = r[cx] - jnp.where(spot, whole, 0.0)

    def applied(ref, i):
        here = ref[i]
        out = diag[i] * here - fx[i] * ref[ahead(i)] - fx[behind(i)] * ref[behind(i)]
        side = fy[i]
        out = out - side * pltpu.roll(here, EY - 1, 1) - pltpu.roll(side * here, 1, 1)
        deep = fz[i]
        return out - deep * pltpu.roll(here, DEPTH - 1, 2) - pltpu.roll(deep * here, 1, 2)

    def begin(i):
        left = r[i] - applied(v, i)
        r[i] = left
        d0[i] = left * inv[i] * (1.0 / THETA)

    over_rows(1, EX - 1, begin)
    ratio = 1.0 / SIGMA
    source, target = d0, d1
    for sweep in range(SWEEPS - 1):
        following = 1.0 / (2.0 * SIGMA - ratio)
        keep, gain = following * ratio, 2.0 * following / DELTA

        def advance(i, source=source, target=target, keep=keep, gain=gain):
            here = source[i]
            left = r[i] - applied(source, i)
            new = v[i] + here
            v[i] = new
            r[i] = left
            target[i] = keep * here + gain * (left * inv[i])

        over_rows(2 + sweep, EX - 2 - sweep, advance)
        ratio = following
        source, target = target, source

    v[HALO - 1] = v[HALO - 1] + source[HALO - 1]
    v[WX + HALO] = v[WX + HALO] + source[WX + HALO]
    squares[...] = jnp.zeros((8, DEPTH), f32)

    def finish(i):
        here = source[i]
        left = r[i] - applied(source, i)
        new = v[i] + here
        v[i] = new
        final[shifted(i)] = new[:, 8:24]
        left = left[:, 8:24]
        left = left * left
        squares[...] += jnp.sum(left[:, :8] + left[:, 8:], axis=0)

    over_rows(HALO, WX + HALO, finish)
    store = pltpu.make_async_copy(final, adjoint, sem)
    store.start()

    def product(i):
        a, p = v[i], phi[i]
        out = (a - v[ahead(i)]) * (p - phi[ahead(i)]) + (a - v[behind(i)]) * (p - phi[behind(i)])
        side = (a - pltpu.roll(a, EY - 1, 1)) * (p - pltpu.roll(p, EY - 1, 1))
        out = out + side + pltpu.roll(side, 1, 1)
        deep = (a - jnp.where(last, 0.0, pltpu.roll(a, DEPTH - 1, 2))) * (
            p - jnp.where(last, 0.0, pltpu.roll(p, DEPTH - 1, 2))
        )
        out = out + deep + jnp.where(first, a * p, pltpu.roll(deep, 1, 2))
        term[shifted(i)] = -0.5 * out[:, 8:24]

    over_rows(HALO, WX + HALO, product)
    store.wait()


def plane_kernel(parts, own, got, out, acc):
    for q in range(LINE):
        total = parts[0, q]
        square = total * total
        for k in range(1, PLANE):
            more = parts[k, q]
            total = total + more
            square = square + more * more
        out[q, 0] = total
        out[q, 1] = square
    acc[...] = own[...] + got[...]


def scale_kernel(sources, parts, out):
    total, square = parts[0, 0], parts[0, 1]
    for q in range(1, LINE):
        total = total + parts[q, 0]
        square = square + parts[q, 1]
    value = total * lax.rsqrt(square / sources + 1.0)
    for q in range(LINE):
        out[q] = value


def spread_kernel(rows, own, got, out, acc):
    value = rows[...]
    for k in range(PLANE):
        out[k] = value
    acc[...] = own[...] + got[...]


def rms_kernel(cells, own, got, rms):
    total = jnp.sum(own[...] + got[...], axis=0, keepdims=True)
    rms[...] = jnp.broadcast_to(
        jnp.sqrt(jnp.sum(total, axis=1, keepdims=True) / cells), (1, DEPTH)
    )


VM = pl.BlockSpec(memory_space=pltpu.VMEM)
SM = pl.BlockSpec(memory_space=pltpu.SMEM)
HB = pl.BlockSpec(memory_space=pl.ANY)


def call(kernel, shapes, specs, *args, scratch=(), limit=48 * 1024 * 1024, outs=None):
    return pl.pallas_call(
        kernel,
        out_shape=[jax.ShapeDtypeStruct(shape, f32) for shape in shapes],
        in_specs=specs,
        out_specs=outs or [VM] * len(shapes),
        scratch_shapes=list(scratch),
        compiler_params=pltpu.CompilerParams(vmem_limit_bytes=limit),
    )(*args)


def body(conductivity, potential, adjoint_guess, observed, receiver_cells, electrodes):
    sources = lax.axis_size("src")
    pot, guess = potential[0], adjoint_guess[0]
    elec = jnp.transpose(electrodes)
    tile = (8, DEPTH)
    swap_x = [(0, 1), (1, 0)]
    (mine,) = call(
        gather_kernel, [(2 * HALO + 2, WY, DEPTH)], [HB] * 5,
        elec, receiver_cells, pot, guess, conductivity,
        scratch=[
            pltpu.SMEM((1, 3), i32),
            pltpu.VMEM((3, NREC), i32),
            pltpu.VMEM((WX, WY, DEPTH), f32),
            pltpu.SemaphoreType.DMA((4 + LOADS,)),
        ],
        limit=GRANT,
    )
    theirs = lax.ppermute(mine, "gx", swap_x)
    faces = (WX // 2, 3, 8, DEPTH)
    up, down, partial = call(
        pack_kernel, [faces, faces, tile], [HB] + [VM] * 3, mine, pot, guess, conductivity,
        scratch=[pltpu.SemaphoreType.DMA],
    )
    ring = lambda step: [(i, (i + step) % 4) for i in range(4)]
    from_low = lax.ppermute(up, "gy", ring(1))
    from_high = lax.ppermute(down, "gy", ring(3))
    (spots,) = call(
        corner_kernel, [(lax.axis_size("gy"), 4, 8, DEPTH)], [VM] * 2, partial, theirs
    )
    spots = lax.all_to_all(spots, "gy", 0, 0, tiled=True)
    block = (WX, WY, DEPTH)
    adjoint, term, squares = call(
        smooth_kernel, [block, block, tile], [VM, SM] + [VM] * 8,
        receiver_cells, elec, observed, pot, guess, conductivity,
        theirs, from_low, from_high, spots,
        scratch=[pltpu.VMEM((EX, EY, DEPTH), f32)] * 11
        + [pltpu.VMEM(block, f32), pltpu.SemaphoreType.DMA],
        outs=[HB, VM, VM],
    )
    planes = [[z * PLANE + k for k in range(PLANE)] for z in range(LINE)]
    lines = [[z * PLANE + k for z in range(LINE)] for k in range(PLANE)]

    def exchange(value, groups):
        return lax.all_to_all(value, "src", 0, 0, axis_index_groups=groups, tiled=True)

    other = lax.ppermute(squares, "gy", [(0, 1), (1, 0), (2, 3), (3, 2)])
    got = exchange(term.reshape(PLANE, LINE, WY, DEPTH), planes)
    sums, squares = call(
        plane_kernel, [(LINE, 2, WY, DEPTH), tile], [VM] * 3, got, squares, other
    )
    got = exchange(sums, lines)
    (scaled,) = call(
        lambda *refs: scale_kernel(sources, *refs), [(LINE, WY, DEPTH)], [VM], got
    )
    other = lax.ppermute(squares, "gx", swap_x)
    got = exchange(scaled, lines)
    spread, squares = call(
        spread_kernel, [(PLANE, LINE, WY, DEPTH), tile], [VM] * 3, got, squares, other
    )
    other = lax.ppermute(squares, "gy", [(0, 2), (2, 0), (1, 3), (3, 1)])
    gradient = exchange(spread, planes).reshape(block)
    cells = WX * lax.axis_size("gx") * WY * lax.axis_size("gy") * DEPTH
    (rms,) = call(
        lambda *refs: rms_kernel(cells, *refs), [(1, DEPTH)], [VM] * 2, squares, other
    )
    return adjoint[None], rms[0, :1], gradient


def solution(mesh):
    return jax.shard_map(
        body,
        mesh=mesh,
        in_specs=(
            P("gx", "gy", None),
            P("src", "gx", "gy", None),
            P("src", "gx", "gy", None),
            P("src", None),
            P(),
            P(None, "src"),
        ),
        out_specs=(P("src", "gx", "gy", None), P("src"), P("gx", "gy", None)),
        check_vma=False,
    )
```
